32 devices in a mesh: groups: 2 (over y), gx: 4 (over z), gy: 2 (over x), col: 2 (over core).
Axes of the slice: x: 2, y: 2, z: 4, core: 2. Of those that a mesh axis runs over, the one named last changes fastest.
Arguments:
- state_in: bfloat16 [64, 2048, 2048], P(('groups', 'col'), 'gx', 'gy'), parts along dimension 0, may hold values from -6 to 6
- tile_class: int32 [256, 128], P(('groups', 'gx'), 'gy'), parts along dimension 0, may hold values from 0 to 7
- class_bias: float32 [8, 32], replicated, may hold values from -4 to 4
- w_point: bfloat16 [32, 32], replicated, may hold values from -1 to 1
- spec_weight: bfloat16 [2, 32, 32, 128, 128], P(None, None, 'col', 'gx', 'gy'), may hold values from -0.75 to 0.75
- grad_out: bfloat16 [64, 2048, 2048], P(('groups', 'col'), 'gx', 'gy'), parts along dimension 0, may hold values from -6 to 6
Outputs:
- act_out: bfloat16 [64, 2048, 2048], P(('groups', 'col'), 'gx', 'gy'), parts along dimension 0
- grad_in: bfloat16 [64, 2048, 2048], P(('groups', 'col'), 'gx', 'gy'), parts along dimension 0
- grad_spec: float32 [4, 32, 32, 128, 128], P('groups', None, 'col', 'gx', 'gy'), parts along dimension 0
- grad_point: float32 [64, 32], P(('groups', 'col')), parts along dimension 0
- grad_bias: float32 [16, 32], P('groups', 'col'), parts along dimension 0
The draws below stay inside these ranges and needn't reach their ends.
There are 2 independent parts, one for each index of `groups`. The reference program is written for one: setup_inputs(seed, part) draws one part's arguments, and reference() takes and returns one part's arrays. A program takes and returns all parts, laid end to end along the dimension named above; an argument that names none is the same for every part. Nothing has to cross between parts.
Inputs may be any that keep to these rules, and one draw needn't show every extreme that they name: `tile_class`: bathymetry class of each 16 x 16 tile of cells.
All inputs are finite; a program needn't handle non-finite values.
Results may differ from the reference program's by a relative error of at most 0.015.
Values may be sent and summed in bfloat16 or wider, within the bound.
No kernel may reach another device: no remote copies, remote signals or barrier semaphores. Data moves between devices by JAX's collectives and lax.ppermute only.
A program may use at most 640 MiB of HBM per device.

```python
import math
import jax
import jax.numpy as jnp
from jax import lax

C = 32
NX = 2048
NY = 2048
MX = 128
MY = 128
TILE = 16
NCLASS = 8
N_GY = 2


def plant(result, stream_key, smallest, largest):
    longest = result.shape.index(max(result.shape))
    spots = []
    for shift in (0, 1):
        where = [jax.random.randint(jax.random.fold_in(stream_key, axis), (), 0, length) for axis, length in enumerate(result.shape)]
        where[longest] = (where[longest] + shift) % result.shape[longest]
        spots.append(tuple(where))
    return result.at[spots[0]].set(smallest).at[spots[1]].set(largest)


def level_of(own_key, extent, cuts, low, largest):
    gain, own = 1.0, jax.random.fold_in(own_key, 6)
    for position, blocks in cuts:
        draws = jnp.exp(jax.random.uniform(jax.random.fold_in(own, position), (blocks,), jnp.float32, low / len(cuts), largest / len(cuts)))
        gain = gain * jnp.repeat(draws, extent[position] // blocks).reshape([-1 if axis == position else 1 for axis in range(len(extent))])
    return gain


def gaussian(key, shape, deviation, bound, split=(), kind=jnp.bfloat16):
    drawn = deviation * jax.random.normal(key, shape, jnp.float32)
    if split:
        drawn = drawn * level_of(key, shape, split, -0.22, 0.18)
    return jnp.clip(drawn, -bound, bound).astype(kind)


def setup_inputs(seed: int = 0, part: int = 0) -> dict:
    keys = jax.random.split(jax.random.key(seed), 7)
    part_splits = jax.random.split(jax.random.fold_in(keys[6], part), 7)
    return {
        "state_in": gaussian(part_splits[0], (C, NX, NY), 1.0, 6.0, ((0, 2), (1, 4), (2, 2))),
        "tile_class": plant(jax.random.randint(part_splits[1], (NX // TILE, NY // TILE), 0, NCLASS), jax.random.fold_in(part_splits[1], 1), 0, NCLASS - 1).astype(jnp.int32),
        "class_bias": gaussian(keys[2], (NCLASS, C), 1.0, 4.0, (), jnp.float32),
        "w_point": gaussian(keys[3], (C, C), C ** -0.5, 1.0),
        "spec_weight": gaussian(keys[4], (2, C, C, MY, MX), (2 * C) ** -0.5, 0.75, ((2, 2), (3, 4), (4, 2))),
        "grad_out": gaussian(part_splits[5], (C, NX, NY), 1.0, 6.0, ((0, 2), (1, 4), (2, 2))),
    }


root_half = 0.7071067811865476
inv_root_tau = 0.3989422804014327

def make_tables():
    freq_y = jnp.arange(MY, dtype=jnp.int32)
    points_y = jnp.arange(NY, dtype=jnp.int32)
    angles_y = (points_y[:, None] * freq_y[None, :] % NY).astype(jnp.float32) * (2.0 * math.pi / NY)
    y_fwd = jnp.stack([jnp.cos(angles_y), -jnp.sin(angles_y)]).astype(jnp.bfloat16)
    angles_t = (freq_y[:, None] * points_y[None, :] % NY).astype(jnp.float32) * (2.0 * math.pi / NY)
    weight_k = jnp.where(freq_y == 0, 1.0, 2.0).astype(jnp.float32)[:, None]
    y_inv = jnp.stack([weight_k * jnp.cos(angles_t), -weight_k * jnp.sin(angles_t)]).astype(jnp.bfloat16)
    freq_x = jnp.arange(MX, dtype=jnp.int32)
    signed_x = jnp.where(freq_x < MX // 2, freq_x, freq_x - MX)
    points_x = jnp.arange(NX, dtype=jnp.int32)
    angles_x = (signed_x[:, None] * points_x[None, :] % NX).astype(jnp.float32) * (2.0 * math.pi / NX)
    cos_part = jnp.cos(angles_x)
    sin_part = jnp.sin(angles_x)
    x_fwd = jnp.stack([jnp.stack([cos_part, -sin_part]), jnp.stack([sin_part, cos_part])]).astype(jnp.bfloat16)
    x_inv = jnp.stack([jnp.stack([cos_part, sin_part]), jnp.stack([-sin_part, cos_part])]).astype(jnp.bfloat16)
    return (y_fwd, y_inv, x_fwd, x_inv)

def mix_modes(weight, spectrum):
    high = lax.Precision.HIGHEST
    real_part = jnp.einsum('iokm,ikm->okm', weight[0], spectrum[0], precision=high) - jnp.einsum('iokm,ikm->okm', weight[1], spectrum[1], precision=high)
    imag_part = jnp.einsum('iokm,ikm->okm', weight[0], spectrum[1], precision=high) + jnp.einsum('iokm,ikm->okm', weight[1], spectrum[0], precision=high)
    return jnp.stack([real_part, imag_part])

def back_mix(weight, grad_modes):
    high = lax.Precision.HIGHEST
    real_part = jnp.einsum('iokm,okm->ikm', weight[0], grad_modes[0], precision=high) + jnp.einsum('iokm,okm->ikm', weight[1], grad_modes[1], precision=high)
    imag_part = jnp.einsum('iokm,okm->ikm', weight[0], grad_modes[1], precision=high) - jnp.einsum('iokm,okm->ikm', weight[1], grad_modes[0], precision=high)
    return jnp.stack([real_part, imag_part])

def weight_grad(spectrum, grad_modes):
    real_part = jnp.einsum('ikm,okm->iokm', spectrum[0], grad_modes[0]) + jnp.einsum('ikm,okm->iokm', spectrum[1], grad_modes[1])
    imag_part = jnp.einsum('ikm,okm->iokm', spectrum[0], grad_modes[1]) - jnp.einsum('ikm,okm->iokm', spectrum[1], grad_modes[0])
    return jnp.stack([real_part, imag_part])

def reference(state_in, tile_class, class_bias, w_point, spec_weight, grad_out):
    y_fwd, y_inv, x_fwd, x_inv = make_tables()
    y_fwd_f = y_fwd.astype(jnp.float32)
    y_inv_f = y_inv.astype(jnp.float32)
    x_fwd_f = x_fwd.astype(jnp.float32)
    x_inv_f = x_inv.astype(jnp.float32)
    scale_fwd = 1.0 / math.sqrt(NX * NY)
    scale_inv = 1.0 / math.sqrt(2.0 * MX * MY)
    state_f = state_in.astype(jnp.float32)
    w_float = w_point.astype(jnp.float32)
    point_mix = jnp.einsum('oi,ixy->oxy', w_float, state_f)
    block_cols = NY // N_GY
    spectrum = jnp.zeros((2, C, MY, MX), jnp.float32)
    for block in range(N_GY):
        lower = block * block_cols
        row_spec = jnp.einsum('cxy,tyk->tckx', state_f[:, :, lower:lower + block_cols], y_fwd_f[:, lower:lower + block_cols]).astype(jnp.bfloat16)
        spectrum = spectrum + jnp.einsum('rckx,rtmx->tckm', row_spec.astype(jnp.float32), x_fwd_f)
    spectrum = spectrum * scale_fwd
    weight_f = spec_weight.astype(jnp.float32)
    mixed = mix_modes(weight_f, spectrum).astype(jnp.bfloat16)
    space_rows = jnp.einsum('rokm,rtmx->tokx', mixed.astype(jnp.float32), x_inv_f).astype(jnp.bfloat16)
    spectral = scale_inv * jnp.einsum('tokx,tky->oxy', space_rows.astype(jnp.float32), y_inv_f)
    one_hot = (tile_class[:, :, None] == jnp.arange(NCLASS, dtype=jnp.int32)).astype(jnp.float32)
    tile_bias = jnp.einsum('abn,no->oab', one_hot, class_bias.astype(jnp.float32))
    tile_rows = NX // TILE
    tile_cols = NY // TILE
    summed = (point_mix + spectral).reshape(C, tile_rows, TILE, tile_cols, TILE)
    pre_act = (summed + tile_bias[:, :, None, :, None]).reshape(C, NX, NY)
    normal_cdf = 0.5 * (1.0 + jax.scipy.special.erf(pre_act * root_half))
    act_out = (pre_act * normal_cdf).astype(jnp.bfloat16)
    gelu_slope = normal_cdf + pre_act * jnp.exp(-0.5 * pre_act * pre_act) * inv_root_tau
    grad_pre = (grad_out.astype(jnp.float32) * gelu_slope).astype(jnp.bfloat16)
    grad_float = grad_pre.astype(jnp.float32)
    grad_point = scale_fwd * jnp.einsum('oxy,ixy->oi', grad_float, state_f)
    tile_sums = grad_float.reshape(C, tile_rows, TILE, tile_cols, TILE).sum(axis=(2, 4))
    grad_bias = scale_fwd * jnp.einsum('abn,oab->no', one_hot, tile_sums)
    grad_modes = jnp.zeros((2, C, MY, MX), jnp.float32)
    for block in range(N_GY):
        lower = block * block_cols
        grad_rows = (scale_inv * jnp.einsum('oxy,tky->tokx', grad_float[:, :, lower:lower + block_cols], y_inv_f[:, :, lower:lower + block_cols])).astype(jnp.bfloat16)
        grad_modes = grad_modes + jnp.einsum('tokx,rtmx->rokm', grad_rows.astype(jnp.float32), x_inv_f)
    grad_spec = weight_grad(spectrum, grad_modes)
    input_modes = back_mix(weight_f, grad_modes).astype(jnp.bfloat16)
    input_rows = (scale_fwd * jnp.einsum('tckm,rtmx->rckx', input_modes.astype(jnp.float32), x_fwd_f)).astype(jnp.bfloat16)
    grad_in = jnp.einsum('oi,oxy->ixy', w_float, grad_float) + jnp.einsum('rckx,ryk->cxy', input_rows.astype(jnp.float32), y_fwd_f)
    return (act_out, grad_in.astype(jnp.bfloat16), grad_spec, grad_point, grad_bias)
```

```python
import functools
import math

import jax
import jax.numpy as jnp
import numpy as np
from jax import lax
from jax.experimental import pallas as pl
from jax.experimental.pallas import tpu as pltpu
from jax.sharding import PartitionSpec as P

TILE = 16
NCLASS = 8
VMEM_BYTES = 44 * 1024 * 1024
MANY = 16

inv_root_two = 0.7071067811865476
inv_root_tau = 0.3989422804014327

f32 = jnp.float32
bf16 = jnp.bfloat16


def dot_nn(a, b):
    return lax.dot_general(a, b, (((1,), (0,)), ((), ())), preferred_element_type=f32)


def dot_nt(a, b):
    return lax.dot_general(a, b, (((1,), (1,)), ((), ())), preferred_element_type=f32)


def dot_tn(a, b):
    return lax.dot_general(a, b, (((0,), (0,)), ((), ())), preferred_element_type=f32)


def params():
    return pltpu.CompilerParams(vmem_limit_bytes=VMEM_BYTES)


def y_table(n_y, m_y, own_k, offset, length, first):
    freq = np.arange(2 * m_y) % m_y
    turns = (freq[:, None] * np.arange(n_y)[None, :]) % n_y * (2.0 * math.pi / n_y)
    whole = np.stack([np.cos(turns), -np.sin(turns)]).astype(bf16)
    own = lax.dynamic_slice(jnp.asarray(whole), (0, first * own_k, offset), (2, m_y, length))
    return own.reshape(2 * m_y, length)


def x_table(n_x, m_x, own_m, offset, length, first):
    freq = np.arange(m_x)
    signed = np.where(freq < m_x // 2, freq, freq - m_x)
    turns = (np.arange(n_x)[:, None] * signed[None, :]) % n_x * (2.0 * math.pi / n_x)
    cos_part = np.cos(turns).reshape(n_x, m_x // own_m, 1, own_m)
    sin_part = np.sin(turns).reshape(n_x, m_x // own_m, 1, own_m)
    real_row = np.concatenate([cos_part, -sin_part], axis=2).reshape(n_x, 2 * m_x)
    imag_row = np.concatenate([sin_part, cos_part], axis=2).reshape(n_x, 2 * m_x)
    whole = np.stack([real_row, imag_row]).astype(bf16)
    whole = np.concatenate([whole, whole], axis=2)
    return lax.dynamic_slice(
        jnp.asarray(whole), (0, offset, first * 2 * own_m), (2, length, 2 * m_x)
    )


def steps_of(sizes):
    return [(a, b) for a in range(sizes[0]) for b in range(sizes[1])]


def pairs_of(sizes, a, b, sign):
    n_gx, n_gy = sizes
    return [
        (g * n_gy + h, ((g + sign * a) % n_gx) * n_gy + (h + sign * b) % n_gy)
        for g in range(n_gx)
        for h in range(n_gy)
    ]


def turn(stacked, sizes, sign):
    n_gx, n_gy = sizes
    grid = stacked.reshape((n_gx, n_gy) + stacked.shape[1:])
    grid = jnp.roll(grid, sign * lax.axis_index("gx"), axis=0)
    grid = jnp.roll(grid, sign * lax.axis_index("gy"), axis=1)
    return grid.reshape(stacked.shape)


def flip(stacked, sizes):
    n_gx, n_gy = sizes
    order = [((-a) % n_gx) * n_gy + (-b) % n_gy for a, b in steps_of(sizes)]
    return stacked[np.array(order)]


def scatter_chunks(chunks, sizes):
    if len(chunks) == 1 and chunks[0].shape[0] > 1:
        placed = turn(chunks[0], sizes, 1)
        arrived = lax.all_to_all(placed, ("gx", "gy"), 0, 0, tiled=True)
        return arrived.astype(f32).sum(axis=0)
    total = None
    arrived = [chunks[0][0]]
    for (a, b), chunk in list(zip(steps_of(sizes), chunks))[1:]:
        arrived.append(lax.ppermute(chunk[0], ("gx", "gy"), pairs_of(sizes, a, b, 1)))
    for piece in arrived:
        total = piece.astype(f32) if total is None else total + piece.astype(f32)
    return total


def gather_chunks(own, sizes):
    if sizes[0] * sizes[1] > MANY:
        stacked = lax.all_gather(own, ("gx", "gy"), axis=0, tiled=False)
        return [turn(stacked, sizes, -1)]
    return [own[None]] + [
        lax.ppermute(own, ("gx", "gy"), pairs_of(sizes, a, b, -1))[None] for a, b in steps_of(sizes)[1:]
    ]


def sum_over_grid(value, sizes):
    if sizes[0] * sizes[1] > MANY:
        return lax.psum(value, ("gx", "gy"))
    total = value
    for a in range(1, sizes[0]):
        pairs = [(g, (g + a) % sizes[0]) for g in range(sizes[0])]
        total = total + lax.ppermute(value, "gx", pairs)
    value = total
    for b in range(1, sizes[1]):
        pairs = [(h, (h + b) % sizes[1]) for h in range(sizes[1])]
        total = total + lax.ppermute(value, "gy", pairs)
    return total


def chunk_shapes(sizes, channels, own_k, lanes):
    count = sizes[0] * sizes[1]
    lengths = [count] if count > MANY else [1] * count
    return [(length, channels, own_k, lanes) for length in lengths]


def chunk_specs(shapes, at=lambda c: c):
    return [
        pl.BlockSpec((s[0], 1) + s[2:], lambda c: (0, at(c), 0, 0)) for s in shapes
    ]


def put_chunks(refs, value, sizes):
    n_gx, n_gy = sizes
    own_k, lanes = value.shape[0] // n_gx, value.shape[1] // n_gy
    per_ref = refs[0].shape[0]
    for place, (a, b) in enumerate(steps_of(sizes)):
        piece = value[a * own_k : (a + 1) * own_k, b * lanes : (b + 1) * lanes]
        refs[place // per_ref][place % per_ref, 0] = piece.astype(bf16)


def take_chunks(refs, sizes):
    n_gx, n_gy = sizes
    per_ref = refs[0].shape[0]

    def chunk(a, b):
        place = a * n_gy + b
        return refs[place // per_ref][place % per_ref, 0].astype(f32)

    rows = [jnp.concatenate([chunk(a, b) for b in range(n_gy)], axis=1) for a in range(n_gx)]
    return jnp.concatenate(rows, axis=0).astype(bf16)


def forward_kernel(sizes, state_ref, y_ref, x_ref, *out_refs):
    half = y_ref.shape[0] // 2
    rows = dot_nt(y_ref[...], state_ref[0]).astype(bf16)
    terms = dot_nn(rows[:half], x_ref[0]) + dot_nn(rows[half:], x_ref[1])
    put_chunks(out_refs, terms, sizes)


def table_specs(y_tab, x_tab):
    return [
        pl.BlockSpec(y_tab.shape, lambda c: (0, 0)),
        pl.BlockSpec(x_tab.shape, lambda c: (0, 0, 0)),
    ]


def forward_modes(state, y_tab, x_tab, sizes, own_k):
    channels, n_rows, n_cols = state.shape
    shapes = chunk_shapes(sizes, channels, own_k, x_tab.shape[2] // sizes[1])
    return pl.pallas_call(
        functools.partial(forward_kernel, sizes),
        grid=(channels,),
        in_specs=[pl.BlockSpec((1, n_rows, n_cols), lambda c: (c, 0, 0))] + table_specs(y_tab, x_tab),
        out_specs=chunk_specs(shapes),
        out_shape=[jax.ShapeDtypeStruct(s, bf16) for s in shapes],
        compiler_params=params(),
        name="forward_modes",
    )(state, y_tab, x_tab)


def gelu_parts(v):
    size = jnp.abs(v)
    bell = jnp.exp2(v * v * (-0.5 * math.log2(math.e)))
    t = 1.0 / (1.0 + (0.3275911 * inv_root_two) * size)
    series = 0.5 * 1.061405429
    for coefficient in (-1.453152027, 1.421413741, -0.284496736, 0.254829592):
        series = series * t + 0.5 * coefficient
    tail = series * t * bell
    cdf = jnp.where(v < 0.0, tail, 1.0 - tail)
    return v * cdf, cdf + v * bell * inv_root_tau


def middle_kernel(sizes, n_chunks, row_step, mix_ref, out_grad_ref, y_ref, x_ref, *refs):
    mode_refs, (act_ref, pre_ref), out_refs = refs[:n_chunks], refs[n_chunks : n_chunks + 2], refs[n_chunks + 2 :]
    modes = take_chunks(mode_refs, sizes)
    n_rows = mix_ref.shape[1]
    half = y_ref.shape[0] // 2
    real_rows = dot_nt(x_ref[0], modes).astype(bf16)
    imag_rows = dot_nt(x_ref[1], modes).astype(bf16)
    space = jnp.concatenate([real_rows, imag_rows], axis=1)
    back = []
    for start in range(0, n_rows, row_step):
        rows = slice(start, start + row_step)
        v = dot_nn(space[rows], y_ref[...]) + mix_ref[0, rows].astype(f32)
        act, slope = gelu_parts(v)
        act_ref[0, rows] = act.astype(bf16)
        pre = (out_grad_ref[0, rows].astype(f32) * slope).astype(bf16)
        pre_ref[0, rows] = pre
        back.append(dot_nt(pre, y_ref[...]).astype(bf16))
    back = jnp.concatenate(back, axis=0)
    terms = dot_tn(back[:, :half], x_ref[0]) + dot_tn(back[:, half:], x_ref[1])
    put_chunks(out_refs, terms, sizes)


def middle(mix, out_grad, y_tab, x_tab, modes, sizes):
    channels, n_rows, n_cols = mix.shape
    field = pl.BlockSpec((1, n_rows, n_cols), lambda c: (c, 0, 0))
    shapes = [m.shape for m in modes]
    results = pl.pallas_call(
        functools.partial(middle_kernel, sizes, len(modes), min(128, n_rows)),
        grid=(channels,),
        in_specs=[field, field] + table_specs(y_tab, x_tab) + chunk_specs(shapes),
        out_specs=[field, field] + chunk_specs(shapes),
        out_shape=[jax.ShapeDtypeStruct(mix.shape, bf16)] * 2 + [jax.ShapeDtypeStruct(s, bf16) for s in shapes],
        compiler_params=params(),
        name="middle",
    )(mix, out_grad, y_tab, x_tab, *modes)
    return results[0], results[1], list(results[2:])


def last_kernel(sizes, point_ref, y_ref, x_ref, *refs):
    modes = take_chunks(refs[:-1], sizes)
    real_rows = dot_nt(x_ref[0], modes).astype(bf16)
    imag_rows = dot_nt(x_ref[1], modes).astype(bf16)
    space = jnp.concatenate([real_rows, imag_rows], axis=1)
    refs[-1][0] = (dot_nn(space, y_ref[...]) + point_ref[0].astype(f32)).astype(bf16)


def last(point_back, y_tab, x_tab, modes, sizes):
    channels, n_rows, n_cols = point_back.shape
    field = pl.BlockSpec((1, n_rows, n_cols), lambda c: (c, 0, 0))
    return pl.pallas_call(
        functools.partial(last_kernel, sizes),
        grid=(channels,),
        in_specs=[field] + table_specs(y_tab, x_tab) + chunk_specs([m.shape for m in modes]),
        out_specs=field,
        out_shape=jax.ShapeDtypeStruct(point_back.shape, bf16),
        compiler_params=params(),
        name="last",
    )(point_back, y_tab, x_tab, *modes)


def spread(weight):
    n_o, n_i = weight.shape
    same = jnp.eye(TILE, dtype=weight.dtype)
    return (weight[:, None, :, None] * same[None, :, None, :]).reshape(n_o * TILE, n_i * TILE)


def point_kernel(n_fields, with_bias, *refs):
    fields, weights = refs[:n_fields], refs[n_fields : 2 * n_fields]
    out_ref = refs[-1]
    channels, n_rows, n_cols = out_ref.shape
    for tile in range(n_rows // TILE):
        rows = slice(tile * TILE, (tile + 1) * TILE)
        total = None
        for field, weight in zip(fields, weights):
            term = dot_nn(weight[...], field[:, rows].reshape(channels * TILE, n_cols))
            total = term if total is None else total + term
        total = total.reshape(channels, TILE, n_cols)
        if with_bias:
            total = total + refs[2 * n_fields][tile][:, None, :]
        out_ref[:, rows] = total.astype(bf16)


def point_map(fields, weights, bias=None):
    channels, n_rows, n_cols = fields[0].shape
    step = min(32, n_rows)
    field = pl.BlockSpec((channels, step, n_cols), lambda r: (0, r, 0))
    in_specs = [field] * len(fields) + [pl.BlockSpec(w.shape, lambda r: (0, 0)) for w in weights]
    extra = []
    if bias is not None:
        in_specs.append(pl.BlockSpec((step // TILE, channels, n_cols), lambda r: (r, 0, 0)))
        extra.append(bias)
    return pl.pallas_call(
        functools.partial(point_kernel, len(fields), bias is not None),
        grid=(n_rows // step,),
        in_specs=in_specs,
        out_specs=field,
        out_shape=jax.ShapeDtypeStruct(fields[0].shape, bf16),
        compiler_params=params(),
        name="point_map",
    )(*fields, *weights, *extra)


def sums_kernel(n_fields, pre_ref, class_ref, *refs):
    fields, outs, bias_ref = refs[:n_fields], refs[n_fields : 2 * n_fields], refs[2 * n_fields]
    channels, n_rows, n_cols = pre_ref.shape

    @pl.when(pl.program_id(0) == 0)
    def _():
        for out in outs:
            out[...] = jnp.zeros_like(out)
        bias_ref[...] = jnp.zeros_like(bias_ref)

    for tile in range(n_rows // TILE):
        rows = slice(tile * TILE, (tile + 1) * TILE)
        pre = pre_ref[:, rows].reshape(channels * TILE, n_cols)
        for field, out in zip(fields, outs):
            out[...] += dot_nt(pre, field[:, rows].reshape(channels * TILE, n_cols))
        bias_ref[...] += dot_nt(pre, class_ref[tile])


def cell_sums(pre, fields, classes):
    channels, n_rows, n_cols = pre.shape
    step = min(32, n_rows)
    field = pl.BlockSpec((channels, step, n_cols), lambda r: (0, r, 0))
    square = channels * TILE
    return pl.pallas_call(
        functools.partial(sums_kernel, len(fields)),
        grid=(n_rows // step,),
        in_specs=[field, pl.BlockSpec((step // TILE, NCLASS, n_cols), lambda r: (r, 0, 0))]
        + [field] * len(fields),
        out_specs=[pl.BlockSpec((square, square), lambda r: (0, 0))] * len(fields)
        + [pl.BlockSpec((square, NCLASS), lambda r: (0, 0))],
        out_shape=[jax.ShapeDtypeStruct((square, square), f32)] * len(fields)
        + [jax.ShapeDtypeStruct((square, NCLASS), f32)],
        compiler_params=params(),
        name="cell_sums",
    )(pre, classes, *fields)


def swap_halves(value):
    half = value.shape[-1] // 2
    return jnp.concatenate([value[..., half:], value[..., :half]], axis=-1)


def on_device(n_gx, n_gy, state_in, tile_class, class_bias, w_point, spec_weight, grad_out):
    sizes = (n_gx, n_gy)
    own_chan, n_rows, n_cols = state_in.shape
    own_k, own_m = spec_weight.shape[3:]
    m_y, m_x = own_k * n_gx, own_m * n_gy
    n_x, n_y = n_rows * n_gx, n_cols * n_gy
    gx_index = lax.axis_index("gx")
    gy_index = lax.axis_index("gy")
    col_index = lax.axis_index("col")
    scale_fwd = 1.0 / math.sqrt(n_x * n_y)
    scale_inv = 1.0 / math.sqrt(2.0 * m_x * m_y)
    other = [(0, 1), (1, 0)]

    state_other = lax.ppermute(state_in, "col", other)
    y_tab = y_table(n_y, m_y, own_k, gy_index * n_cols, n_cols, gx_index)
    x_tab = x_table(n_x, m_x, own_m, gx_index * n_rows, n_rows, gy_index)
    k_weight = jnp.where(
        (jnp.arange(own_k) + gx_index * own_k) == 0, scale_inv, 2.0 * scale_inv
    ).astype(f32)[None, :, None]

    terms = forward_modes(state_in, y_tab, x_tab, sizes, own_k)
    spectrum = (scatter_chunks(terms, sizes) * scale_fwd).astype(bf16)
    spectrum_other = lax.ppermute(spectrum, "col", other)

    w_real = jnp.concatenate([spec_weight[0], spec_weight[0]], axis=-1)
    w_imag = jnp.concatenate([-spec_weight[1], spec_weight[1]], axis=-1)

    first = col_index == 0
    spec_all = jnp.concatenate(
        [jnp.where(first, spectrum, spectrum_other), jnp.where(first, spectrum_other, spectrum)], axis=0
    ).astype(f32)
    mixed = jnp.sum(
        w_real.astype(f32) * spec_all[:, None] + w_imag.astype(f32) * swap_halves(spec_all)[:, None], axis=0
    )
    mixed_all = gather_chunks((mixed * k_weight).astype(bf16), sizes)

    w_rows = lax.dynamic_slice_in_dim(w_point, col_index * own_chan, own_chan, 0)
    w_cols = lax.dynamic_slice_in_dim(w_point, col_index * own_chan, own_chan, 1)
    own_cols = lax.dynamic_slice_in_dim(w_rows, col_index * own_chan, own_chan, 1)
    other_cols = lax.dynamic_slice_in_dim(w_rows, (1 - col_index) * own_chan, own_chan, 1)
    other_rows = lax.dynamic_slice_in_dim(w_cols, (1 - col_index) * own_chan, own_chan, 0)
    tile_rows, tile_cols = tile_class.shape
    one_hot = (tile_class[:, None, :] == jnp.arange(NCLASS, dtype=jnp.int32)[None, :, None]).astype(f32)
    widen = jnp.asarray(np.repeat(np.eye(tile_cols), TILE, axis=1).astype(np.float32))
    bias_own = lax.dynamic_slice_in_dim(class_bias, col_index * own_chan, own_chan, 1)
    high = lax.Precision.HIGHEST
    tile_bias = jnp.sum(one_hot[:, :, None, :] * bias_own[None, :, :, None], axis=1)
    bias = jnp.dot(tile_bias.reshape(tile_rows * own_chan, tile_cols), widen, precision=high)
    bias = bias.reshape(tile_rows, own_chan, n_cols)
    classes = jnp.dot(
        one_hot.astype(bf16).reshape(tile_rows * NCLASS, tile_cols), widen.astype(bf16), preferred_element_type=f32
    )
    classes = classes.astype(bf16).reshape(tile_rows, NCLASS, n_cols)
    mix = point_map([state_in, state_other], [spread(own_cols), spread(other_cols)], bias)

    act_out, grad_pre, back_terms = middle(mix, grad_out, y_tab, x_tab, mixed_all, sizes)
    pre_other = lax.ppermute(grad_pre, "col", other)
    grad_modes = scatter_chunks(back_terms, sizes) * k_weight

    input_terms = jnp.sum(
        w_real.astype(f32) * grad_modes[None] - w_imag.astype(f32) * swap_halves(grad_modes)[None], axis=1
    )
    lower, upper = input_terms[:own_chan], input_terms[own_chan:]
    input_modes = jnp.where(first, lower, upper) + lax.ppermute(jnp.where(first, upper, lower), "col", other)
    input_all = gather_chunks((input_modes * scale_fwd).astype(bf16), sizes)

    s_real, s_imag = spec_all[:, None, :, :own_m], spec_all[:, None, :, own_m:]
    g_real, g_imag = grad_modes[None, :, :, :own_m], grad_modes[None, :, :, own_m:]
    grad_spec = jnp.stack([g_real * s_real + g_imag * s_imag, g_imag * s_real - g_real * s_imag])

    own_square, other_square, bias_sums = cell_sums(grad_pre, [state_in, state_other], classes)

    def trace(square):
        parts = square.reshape(own_chan, TILE, own_chan, TILE)
        return jnp.sum(parts * jnp.eye(TILE, dtype=f32)[None, :, None, :], axis=(1, 3))

    sums = jnp.concatenate(
        [trace(own_square), trace(other_square), bias_sums.reshape(own_chan, TILE, NCLASS).sum(axis=1)], axis=1
    )
    sums = sum_over_grid(sums * scale_fwd, sizes)
    own_part, other_part = sums[:, :own_chan], sums[:, own_chan : 2 * own_chan]
    grad_point = jnp.where(
        col_index == 0,
        jnp.concatenate([own_part, other_part], axis=1),
        jnp.concatenate([other_part, own_part], axis=1),
    )
    grad_bias = sums[:, 2 * own_chan :].T

    own_rows = lax.dynamic_slice_in_dim(w_cols, col_index * own_chan, own_chan, 0)
    point_back = point_map([grad_pre, pre_other], [spread(own_rows.T), spread(other_rows.T)])
    grad_in = last(point_back, y_tab, x_tab, input_all, sizes)
    return (act_out, grad_in, grad_spec, grad_point, grad_bias)


def solution(mesh):
    return jax.shard_map(
        functools.partial(on_device, mesh.shape["gx"], mesh.shape["gy"]),
        mesh=mesh,
        in_specs=(
            P(("groups", "col"), "gx", "gy"),
            P(("groups", "gx"), "gy"),
            P(),
            P(),
            P(None, None, "col", "gx", "gy"),
            P(("groups", "col"), "gx", "gy"),
        ),
        out_specs=(
            P(("groups", "col"), "gx", "gy"),
            P(("groups", "col"), "gx", "gy"),
            P("groups", None, "col", "gx", "gy"),
            P(("groups", "col"), None),
            P("groups", "col"),
        ),
        check_vma=False,
    )
```

```python
import functools
import math

import jax
import jax.numpy as jnp
import numpy as np
from jax import lax
from jax.experimental import pallas as pl
from jax.experimental.pallas import tpu as pltpu
from jax.sharding import PartitionSpec as P

TILE = 16
NCLASS = 8
VMEM_BYTES = 48 * 1024 * 1024
SPLITS = 2

inv_root_two = 0.7071067811865476
inv_root_tau = 0.3989422804014327

f32 = jnp.float32
bf16 = jnp.bfloat16


def dot_nn(a, b):
    return lax.dot_general(a, b, (((1,), (0,)), ((), ())), preferred_element_type=f32)


def dot_nt(a, b):
    return lax.dot_general(a, b, (((1,), (1,)), ((), ())), preferred_element_type=f32)


def dot_tn(a, b):
    return lax.dot_general(a, b, (((0,), (0,)), ((), ())), preferred_element_type=f32)


def params():
    return pltpu.CompilerParams(vmem_limit_bytes=VMEM_BYTES)


def cost(flops, *arrays, transcendentals=0):
    size = sum(math.prod(a.shape) * jnp.dtype(a.dtype).itemsize for a in arrays)
    return pl.CostEstimate(flops=int(flops), bytes_accessed=int(size), transcendentals=int(transcendentals))


def divisor(length, limit):
    return max(d for d in range(1, limit + 1) if length % d == 0)


def y_table(n_y, m_y, offset, length):
    turns = (np.arange(m_y)[:, None] * np.arange(n_y)[None, :]) % n_y * (2.0 * math.pi / n_y)
    whole = np.concatenate([np.cos(turns), -np.sin(turns)]).astype(bf16)
    return lax.dynamic_slice_in_dim(jnp.asarray(whole), offset, length, 1)


def x_table(n_x, m_x, own_m, offset, length):
    freq = np.arange(m_x)
    signed = np.where(freq < m_x // 2, freq, freq - m_x)
    turns = (np.arange(n_x)[:, None] * signed[None, :]) % n_x * (2.0 * math.pi / n_x)
    cos_part = np.cos(turns).reshape(n_x, m_x // own_m, 1, own_m)
    sin_part = np.sin(turns).reshape(n_x, m_x // own_m, 1, own_m)
    real_row = np.concatenate([cos_part, -sin_part], axis=2).reshape(n_x, 2 * m_x)
    imag_row = np.concatenate([sin_part, cos_part], axis=2).reshape(n_x, 2 * m_x)
    whole = np.stack([real_row, imag_row]).astype(bf16)
    return lax.dynamic_slice_in_dim(jnp.asarray(whole), offset, length, 1)


def exchange(chunks):
    return lax.all_to_all(chunks, ("gx", "gy"), 0, 0, tiled=True)


def put_chunks(ref, channel, value, n_gy):
    own_k, lanes = ref.shape[2:]
    for place in range(ref.shape[0]):
        a, b = divmod(place, n_gy)
        piece = value[a * own_k : (a + 1) * own_k, b * lanes : (b + 1) * lanes]
        ref[place, channel] = piece.astype(bf16)


def take_chunks(ref, channel, n_gy):
    own_k, lanes = ref.shape[2:]
    kind = bf16 if own_k % 16 == 0 and lanes % 128 == 0 else f32
    rows = [
        jnp.concatenate([ref[a + b, channel].astype(kind) for b in range(n_gy)], axis=1)
        for a in range(0, ref.shape[0], n_gy)
    ]
    return jnp.concatenate(rows, axis=0).astype(bf16)


def rows_of_modes(modes, x_ref):
    return [dot_nt(x_ref[part], modes).astype(bf16) for part in range(2)]


def forward_kernel(n_gy, state_ref, y_ref, x_ref, out_ref):
    half = y_ref.shape[0] // 2
    for c in range(state_ref.shape[0]):
        rows = dot_nt(y_ref[...], state_ref[c]).astype(bf16)
        terms = dot_nn(rows[:half], x_ref[0]) + dot_nn(rows[half:], x_ref[1])
        put_chunks(out_ref, c, terms, n_gy)


def table_specs(y_tab, x_tab):
    return [
        pl.BlockSpec(y_tab.shape, lambda c: (0, 0)),
        pl.BlockSpec(x_tab.shape, lambda c: (0, 0, 0)),
    ]


def transform_flops(channels, y_tab, x_tab):
    n_rows, wide = x_tab.shape[1:]
    return 2 * channels * n_rows * (y_tab.shape[0] * y_tab.shape[1] + y_tab.shape[0] * wide)


def forward_modes(state, y_tab, x_tab, sizes, own_k):
    channels, n_rows, n_cols = state.shape
    out = jax.ShapeDtypeStruct((sizes[0] * sizes[1], channels, own_k, x_tab.shape[2] // sizes[1]), bf16)
    step = divisor(channels, 4)
    return pl.pallas_call(
        functools.partial(forward_kernel, sizes[1]),
        grid=(channels // step,),
        in_specs=[pl.BlockSpec((step, n_rows, n_cols), lambda c: (c, 0, 0))] + table_specs(y_tab, x_tab),
        out_specs=pl.BlockSpec((out.shape[0], step) + out.shape[2:], lambda c: (0, c, 0, 0)),
        out_shape=out,
        compiler_params=params(),
        cost_estimate=cost(transform_flops(channels, y_tab, x_tab), state, out),
        name="forward_modes",
    )(state, y_tab, x_tab)


def gelu_parts(v):
    v = v.astype(bf16)
    half = jnp.asarray(0.5, bf16)
    bell = jnp.exp2(v * v * jnp.asarray(-0.5 * math.log2(math.e), bf16)) * jnp.asarray(inv_root_tau, bf16)
    cdf = lax.erf(v * jnp.asarray(inv_root_two, bf16)).astype(bf16) * half + half
    return v * cdf, cdf + v * bell


def middle_kernel(n_gy, row_step, mix_ref, out_grad_ref, y_ref, x_ref, mode_ref, *refs):
    act_ref, pre_ref, out_ref = refs[-3:]
    n_rows = mix_ref.shape[1]
    half = y_ref.shape[0] // 2
    for c in range(mix_ref.shape[0]):
        space = jnp.concatenate(rows_of_modes(take_chunks(mode_ref, c, n_gy), x_ref), axis=1)
        back = []
        for start in range(0, n_rows, row_step):
            rows = slice(start, start + row_step)
            v = dot_nn(space[rows], y_ref[...]) + mix_ref[c, rows].astype(f32)
            act, slope = gelu_parts(v)
            act_ref[c, rows] = act
            pre = out_grad_ref[c, rows] * slope
            pre_ref[c, rows] = pre
            back.append(dot_nt(pre, y_ref[...]).astype(bf16))
        back = jnp.concatenate(back, axis=0)
        terms = dot_tn(back[:, :half], x_ref[0]) + dot_tn(back[:, half:], x_ref[1])
        put_chunks(out_ref, c, terms, n_gy)


def middle(mix, out_grad, y_tab, x_tab, modes, sizes, first=0, before=()):
    channels, n_rows, n_cols = mix.shape
    step = divisor(modes.shape[1], 2)
    skip = first // step
    field = pl.BlockSpec((step, n_rows, n_cols), lambda c: (c + skip, 0, 0))
    chunk = (modes.shape[0], step) + modes.shape[2:]
    chunks = jax.ShapeDtypeStruct((modes.shape[0], channels) + modes.shape[2:], bf16)
    flops = 2 * transform_flops(modes.shape[1], y_tab, x_tab)
    moved = jax.ShapeDtypeStruct((4 * modes.shape[1], n_rows, n_cols), bf16)
    return pl.pallas_call(
        functools.partial(middle_kernel, sizes[1], min(256, n_rows)),
        grid=(modes.shape[1] // step,),
        in_specs=[field, field]
        + table_specs(y_tab, x_tab)
        + [pl.BlockSpec(chunk, lambda c: (0, c, 0, 0))]
        + [pl.BlockSpec(memory_space=pl.ANY)] * len(before),
        out_specs=[field, field, pl.BlockSpec(chunk, lambda c: (0, c + skip, 0, 0))],
        out_shape=[jax.ShapeDtypeStruct(mix.shape, bf16)] * 2 + [chunks],
        input_output_aliases={5 + n: n for n in range(len(before))},
        compiler_params=params(),
        cost_estimate=cost(flops, moved),
        name="middle",
    )(mix, out_grad, y_tab, x_tab, modes, *before)


def last_kernel(n_gy, point_ref, y_ref, x_ref, mode_ref, out_ref):
    for c in range(point_ref.shape[0]):
        space = jnp.concatenate(rows_of_modes(take_chunks(mode_ref, c, n_gy), x_ref), axis=1)
        out_ref[c] = (dot_nn(space, y_ref[...]) + point_ref[c].astype(f32)).astype(bf16)


def last(point_back, y_tab, x_tab, modes, sizes):
    channels, n_rows, n_cols = point_back.shape
    step = divisor(channels, 4)
    field = pl.BlockSpec((step, n_rows, n_cols), lambda c: (c, 0, 0))
    return pl.pallas_call(
        functools.partial(last_kernel, sizes[1]),
        grid=(channels // step,),
        in_specs=[field]
        + table_specs(y_tab, x_tab)
        + [pl.BlockSpec((modes.shape[0], step) + modes.shape[2:], lambda c: (0, c, 0, 0))],
        out_specs=field,
        out_shape=jax.ShapeDtypeStruct(point_back.shape, bf16),
        compiler_params=params(),
        cost_estimate=cost(transform_flops(channels, y_tab, x_tab), point_back, point_back),
        name="last",
    )(point_back, y_tab, x_tab, modes)


def chooser(rows, columns, first):
    channel = lax.broadcasted_iota(jnp.int32, (rows, columns), 0) // TILE + first
    return channel == lax.broadcasted_iota(jnp.int32, (rows, columns), 1)


def same_row(rows, columns):
    return lax.broadcasted_iota(jnp.int32, (rows, columns), 0) % TILE == (
        lax.broadcasted_iota(jnp.int32, (rows, columns), 1) % TILE
    )


def spread(weight, out_first, in_first, wide, transposed):
    channels = weight.shape[0]
    picks_out = chooser(wide, channels, out_first).astype(bf16)
    picks_in = chooser(wide, channels, in_first).astype(bf16)
    half = dot_nt(picks_out, weight) if transposed else dot_nn(picks_out, weight)
    return jnp.where(same_row(wide, wide), dot_nt(half.astype(bf16), picks_in), 0.0).astype(bf16)


def point_kernel(transposed, where_ref, own_ref, other_ref, weight_ref, *refs):
    bias_ref, (out_ref, spread_ref) = refs[:-2], refs[-2:]
    channels, n_rows, n_cols = out_ref.shape
    wide = channels * TILE

    @pl.when(pl.program_id(0) == 0)
    def _():
        own = where_ref[0] * channels
        for n, first in enumerate((own, channels - own)):
            spread_ref[n] = spread(weight_ref[...], own, first, wide, transposed)

    for tile in range(n_rows // TILE):
        rows = slice(tile * TILE, (tile + 1) * TILE)
        total = dot_nn(spread_ref[0], own_ref[:, rows].reshape(wide, n_cols))
        total = total + dot_nn(spread_ref[1], other_ref[:, rows].reshape(wide, n_cols))
        total = total.reshape(channels, TILE, n_cols)
        for ref in bias_ref:
            total = total + ref[tile][:, None, :]
        out_ref[:, rows] = total.astype(bf16)


def over_rows(kernel, where, fields, others, other_specs, out_specs, out_shape, scratch, step, flops, name):
    channels, n_rows, n_cols = fields[0].shape
    field = pl.BlockSpec((channels, step, n_cols), lambda r, w: (0, r, 0))
    outs = out_shape if isinstance(out_shape, list) else [out_shape]
    return pl.pallas_call(
        kernel,
        grid_spec=pltpu.PrefetchScalarGridSpec(
            num_scalar_prefetch=1,
            grid=(n_rows // step,),
            in_specs=[field] * len(fields) + other_specs,
            out_specs=out_specs,
            scratch_shapes=scratch,
        ),
        out_shape=out_shape,
        compiler_params=params(),
        cost_estimate=cost(flops, *fields, *others, *outs),
        name=name,
    )(where, *fields, *others)


def whole_spec(array):
    return pl.BlockSpec(array.shape, lambda r, w: (0,) * array.ndim)


def row_step(n_rows, limit):
    return TILE * divisor(n_rows // TILE, limit // TILE)


def point_mixing(where, fields, weight, transposed, bias=()):
    channels, n_rows, n_cols = fields[0].shape
    step = row_step(n_rows, 128)
    wide = channels * TILE
    return over_rows(
        functools.partial(point_kernel, transposed),
        where,
        fields,
        [weight, *bias],
        [whole_spec(weight)]
        + [pl.BlockSpec((step // TILE, channels, n_cols), lambda r, w: (r, 0, 0)) for _ in bias],
        pl.BlockSpec((channels, step, n_cols), lambda r, w: (0, r, 0)),
        jax.ShapeDtypeStruct(fields[0].shape, bf16),
        [pltpu.VMEM((2, wide, wide), bf16)],
        step,
        4 * wide * wide * n_cols * (n_rows // TILE),
        "point_mixing",
    )


def sums_kernel(scale, where_ref, pre_ref, own_ref, other_ref, class_ref, out_ref, square_ref, bias_ref):
    channels, n_rows, n_cols = pre_ref.shape
    wide = channels * TILE
    step, last_step = pl.program_id(0), pl.num_programs(0) - 1

    @pl.when(step == 0)
    def _():
        square_ref[...] = jnp.zeros_like(square_ref)
        bias_ref[...] = jnp.zeros_like(bias_ref)

    for tile in range(n_rows // TILE):
        rows = slice(tile * TILE, (tile + 1) * TILE)
        pre = pre_ref[:, rows].reshape(wide, n_cols)
        square_ref[0] += dot_nt(pre, own_ref[:, rows].reshape(wide, n_cols))
        square_ref[1] += dot_nt(pre, other_ref[:, rows].reshape(wide, n_cols))
        bias_ref[...] += dot_nt(pre, class_ref[tile])

    @pl.when(step == last_step)
    def _():
        own = where_ref[0] * channels
        lanes = out_ref.shape[1]
        high = lax.Precision.HIGHEST
        total = jnp.zeros((wide, lanes), f32)
        for n, first in enumerate((own, channels - own)):
            kept = jnp.where(same_row(wide, wide), square_ref[n], 0.0)
            total = total + jnp.dot(kept, chooser(wide, lanes, first).astype(f32), precision=high)
        shift = lax.broadcasted_iota(jnp.int32, (NCLASS, lanes), 0) + 2 * channels
        shift = (shift == lax.broadcasted_iota(jnp.int32, (NCLASS, lanes), 1)).astype(f32)
        total = total + jnp.dot(bias_ref[...], shift, precision=high)
        out_ref[...] = total.reshape(channels, TILE, lanes).sum(axis=1) * scale


def cell_sums(where, pre, state_own, state_other, classes, scale):
    channels, n_rows, n_cols = pre.shape
    step = row_step(n_rows, 64)
    wide = channels * TILE
    return over_rows(
        functools.partial(sums_kernel, scale),
        where,
        [pre, state_own, state_other],
        [classes],
        [pl.BlockSpec((step // TILE, NCLASS, n_cols), lambda r, w: (r, 0, 0))],
        pl.BlockSpec((channels, 128), lambda r, w: (0, 0)),
        jax.ShapeDtypeStruct((channels, 128), f32),
        [pltpu.VMEM((2, wide, wide), f32), pltpu.VMEM((wide, NCLASS), f32)],
        step,
        4 * wide * wide * n_cols * (n_rows // TILE),
        "cell_sums",
    )


def mode_weight(where_ref, own_k, scale):
    k = where_ref[1] * own_k + lax.broadcasted_iota(jnp.int32, (own_k, 1), 0)
    return jnp.where(k == 0, scale, 2.0 * scale).astype(f32)


def swap_parts(value):
    half = value.shape[-1] // 2
    return jnp.concatenate([value[..., half:], value[..., :half]], axis=-1)


def widen_kernel(weight_ref, real_ref, imag_ref):
    real_part, imag_part = weight_ref[0], weight_ref[1]
    real_ref[...] = jnp.concatenate([real_part, real_part], axis=-1)
    imag_ref[...] = jnp.concatenate([-imag_part, imag_part], axis=-1)


def widen_weights(weight):
    n_in, n_out, own_k, own_m = weight.shape[1:]
    step = divisor(n_in, 4)
    out = jax.ShapeDtypeStruct((n_in, n_out, own_k, 2 * own_m), bf16)
    out_spec = pl.BlockSpec((step, n_out, own_k, 2 * own_m), lambda i: (i, 0, 0, 0))
    return pl.pallas_call(
        widen_kernel,
        grid=(n_in // step,),
        in_specs=[pl.BlockSpec((2, step, n_out, own_k, own_m), lambda i: (0, i, 0, 0, 0))],
        out_specs=[out_spec, out_spec],
        out_shape=[out, out],
        compiler_params=params(),
        cost_estimate=cost(0, weight, weight, out, out),
        name="widen_weights",
    )(weight)


def mix_kernel(scale, where_ref, real_ref, imag_ref, own_ref, other_ref, out_ref, spec_ref, swap_ref):
    channels, own_k, lanes = own_ref.shape

    @pl.when(pl.program_id(0) == 0)
    def _():
        own = where_ref[0] * channels
        for source, first in ((own_ref, own), (other_ref, channels - own)):
            for c in range(channels):
                value = source[c].astype(f32)
                spec_ref[first + c] = value
                swap_ref[first + c] = swap_parts(value)

    factor = mode_weight(where_ref, own_k, scale)
    for o in range(real_ref.shape[1]):
        total = jnp.zeros((own_k, lanes), f32)
        for i in range(2 * channels):
            total = total + (
                real_ref[i, o].astype(f32) * spec_ref[i] + imag_ref[i, o].astype(f32) * swap_ref[i]
            )
        value = (total * factor).astype(bf16)
        for place in range(out_ref.shape[0]):
            out_ref[place, o] = value


def mix_modes(where, w_real, w_imag, own, other, copies, scale, first, count):
    n_in, n_out, own_k, lanes = w_real.shape
    step = divisor(count, 4)
    skip = first // step
    spec = pl.BlockSpec(own.shape, lambda o, w: (0, 0, 0))
    weight = pl.BlockSpec((n_in, step, own_k, lanes), lambda o, w: (0, o + skip, 0, 0))
    return pl.pallas_call(
        functools.partial(mix_kernel, scale),
        grid_spec=pltpu.PrefetchScalarGridSpec(
            num_scalar_prefetch=1,
            grid=(count // step,),
            in_specs=[weight, weight, spec, spec],
            out_specs=pl.BlockSpec((copies, step, own_k, lanes), lambda o, w: (0, o, 0, 0)),
            scratch_shapes=[pltpu.VMEM((n_in, own_k, lanes), f32)] * 2,
        ),
        out_shape=jax.ShapeDtypeStruct((copies, count, own_k, lanes), bf16),
        compiler_params=params(),
        cost_estimate=cost(4 * n_in * count * own_k * lanes, w_real, w_imag),
        name="mix_modes",
    )(where, w_real, w_imag, own, other)


def sum_chunks(where_ref, chunk_refs, scale):
    own_k = chunk_refs[0].shape[2]
    factor = mode_weight(where_ref, own_k, scale)
    for ref in chunk_refs:
        for channel in range(ref.shape[1]):
            total = ref[0, channel].astype(f32)
            for place in range(1, ref.shape[0]):
                total = total + ref[place, channel].astype(f32)
            yield total * factor


def back_kernel(scale, scale_out, n_chunks, where_ref, real_ref, imag_ref, *refs):
    out_ref, grad_ref, swap_ref = refs[n_chunks:]

    @pl.when(pl.program_id(0) == 0)
    def _():
        for o, value in enumerate(sum_chunks(where_ref, refs[:n_chunks], scale)):
            grad_ref[o] = value
            swap_ref[o] = swap_parts(value)

    for i in range(real_ref.shape[0]):
        total = jnp.zeros(out_ref.shape[1:], f32)
        for o in range(real_ref.shape[1]):
            total = total + (
                real_ref[i, o].astype(f32) * grad_ref[o] - imag_ref[i, o].astype(f32) * swap_ref[o]
            )
        out_ref[i] = total * scale_out


def back_mix(where, w_real, w_imag, chunks, scale, scale_out):
    n_in, n_out, own_k, lanes = w_real.shape
    step = divisor(n_in // 2, 8)
    blocks = n_in // step
    half = blocks // 2
    weight = pl.BlockSpec((step, n_out, own_k, lanes), lambda i, w: ((i + (1 - w[0]) * half) % blocks, 0, 0, 0))
    return pl.pallas_call(
        functools.partial(back_kernel, scale, scale_out, len(chunks)),
        grid_spec=pltpu.PrefetchScalarGridSpec(
            num_scalar_prefetch=1,
            grid=(blocks,),
            in_specs=[weight, weight] + [pl.BlockSpec(c.shape, lambda i, w: (0, 0, 0, 0)) for c in chunks],
            out_specs=pl.BlockSpec((step, own_k, lanes), lambda i, w: (i, 0, 0)),
            scratch_shapes=[pltpu.VMEM((n_out, own_k, lanes), f32)] * 2,
        ),
        out_shape=jax.ShapeDtypeStruct((n_in, own_k, lanes), f32),
        compiler_params=params(),
        cost_estimate=cost(4 * n_in * n_out * own_k * lanes, w_real, w_imag),
        name="back_mix",
    )(where, w_real, w_imag, *chunks)


def weight_kernel(scale, n_chunks, where_ref, spec_ref, *refs):
    out_ref, real_ref, imag_ref = refs[n_chunks:]
    n_out, own_k, own_m = real_ref.shape

    @pl.when(pl.program_id(0) == 0)
    def _():
        for o, value in enumerate(sum_chunks(where_ref, refs[:n_chunks], scale)):
            real_ref[o] = value[:, :own_m]
            imag_ref[o] = value[:, own_m:]

    for i in range(out_ref.shape[1]):
        value = spec_ref[i].astype(f32)
        s_real, s_imag = value[:, :own_m], value[:, own_m:]
        for o in range(n_out):
            g_real, g_imag = real_ref[o], imag_ref[o]
            out_ref[0, i, o] = g_real * s_real + g_imag * s_imag
            out_ref[1, i, o] = g_imag * s_real - g_real * s_imag


def weight_grad(where, chunks, spec_all, n_out, scale):
    n_in, own_k, lanes = spec_all.shape
    own_m = lanes // 2
    step = divisor(n_in, 4)
    out = jax.ShapeDtypeStruct((2, n_in, n_out, own_k, own_m), f32)
    return pl.pallas_call(
        functools.partial(weight_kernel, scale, len(chunks)),
        grid_spec=pltpu.PrefetchScalarGridSpec(
            num_scalar_prefetch=1,
            grid=(n_in // step,),
            in_specs=[pl.BlockSpec((step, own_k, lanes), lambda i, w: (i, 0, 0))]
            + [pl.BlockSpec(c.shape, lambda i, w: (0, 0, 0, 0)) for c in chunks],
            out_specs=pl.BlockSpec((2, step, n_out, own_k, own_m), lambda i, w: (0, i, 0, 0, 0)),
            scratch_shapes=[pltpu.VMEM((n_out, own_k, own_m), f32)] * 2,
        ),
        out_shape=out,
        compiler_params=params(),
        cost_estimate=cost(6 * n_in * n_out * own_k * own_m, out, out),
        name="weight_grad",
    )(where, spec_all, *chunks)


def slabs_of(value, shape):
    high = lax.reduce_precision(value, 8, 7)
    middle_part = lax.reduce_precision(value - high, 8, 7)
    parts = jnp.stack([high, middle_part, value - high - middle_part]).astype(bf16).reshape(-1)
    size = math.prod(shape)
    count = -(-parts.shape[0] // size)
    return jnp.pad(parts, (0, count * size - parts.shape[0])).reshape((count,) + shape)


def sum_of_slabs(slabs, shape):
    total = slabs.astype(f32).sum(axis=0).reshape(-1)
    return total[: 3 * math.prod(shape)].reshape((3,) + shape).sum(axis=0)


def on_device(n_gx, n_gy, state_in, tile_class, class_bias, w_point, spec_weight, grad_out):
    sizes = (n_gx, n_gy)
    n_grid = n_gx * n_gy
    own_chan, n_rows, n_cols = state_in.shape
    own_k, own_m = spec_weight.shape[3:]
    m_y, m_x = own_k * n_gx, own_m * n_gy
    n_x, n_y = n_rows * n_gx, n_cols * n_gy
    gx_index = lax.axis_index("gx")
    gy_index = lax.axis_index("gy")
    col_index = lax.axis_index("col")
    scale_fwd = 1.0 / math.sqrt(n_x * n_y)
    scale_inv = 1.0 / math.sqrt(2.0 * m_x * m_y)
    other = [(0, 1), (1, 0)]
    where = jnp.stack([col_index, gx_index]).astype(jnp.int32)

    state_other = lax.ppermute(state_in, "col", other)
    y_tab = y_table(n_y, m_y, gy_index * n_cols, n_cols)
    x_tab = x_table(n_x, m_x, own_m, gx_index * n_rows, n_rows)

    w_real, w_imag = widen_weights(spec_weight)

    tile_rows, tile_cols = tile_class.shape
    one_hot = (tile_class[:, None, :] == jnp.arange(NCLASS, dtype=jnp.int32)[None, :, None]).astype(f32)
    widen = jnp.asarray(np.repeat(np.eye(tile_cols), TILE, axis=1).astype(np.float32))
    bias_own = lax.dynamic_slice_in_dim(class_bias, col_index * own_chan, own_chan, 1)
    tile_bias = jnp.sum(one_hot[:, :, None, :] * bias_own[None, :, :, None], axis=1)
    bias = jnp.dot(
        tile_bias.reshape(tile_rows * own_chan, tile_cols), widen, precision=lax.Precision.HIGHEST
    ).reshape(tile_rows, own_chan, n_cols)
    classes = jnp.dot(
        one_hot.astype(bf16).reshape(tile_rows * NCLASS, tile_cols), widen.astype(bf16), preferred_element_type=f32
    )
    classes = classes.astype(bf16).reshape(tile_rows, NCLASS, n_cols)
    mix = point_mixing(where, [state_in, state_other], w_point, False, [bias])

    terms = exchange(forward_modes(state_in, y_tab, x_tab, sizes, own_k))
    terms, mix, w_real, w_imag = lax.optimization_barrier((terms, mix, w_real, w_imag))
    spectrum = (terms.astype(f32).sum(axis=0) * scale_fwd).astype(bf16)
    spectrum_other = lax.ppermute(spectrum, "col", other)
    halves = SPLITS if own_chan % SPLITS == 0 else 1
    count = own_chan // halves
    mixed = [
        exchange(
            mix_modes(where, w_real, w_imag, spectrum, spectrum_other, n_grid, scale_inv, n * count, count)
        )
        for n in range(halves)
    ]

    done = ()
    for n in range(halves):
        done = middle(mix, grad_out, y_tab, x_tab, mixed[n], sizes, n * count, done)
    act_out, grad_pre, back_terms = done
    back_terms = [exchange(back_terms)]
    pre_other = lax.ppermute(grad_pre, "col", other)

    sums = cell_sums(where, grad_pre, state_in, state_other, classes, scale_fwd)
    sums, *back_terms = lax.optimization_barrier((sums, *back_terms))

    input_terms = back_mix(where, w_real, w_imag, back_terms, scale_inv, scale_fwd)
    input_modes = input_terms[own_chan:] + lax.ppermute(input_terms[:own_chan], "col", other)
    sent = jnp.concatenate([input_modes.astype(bf16), slabs_of(sums, input_modes.shape[1:])], axis=0)
    arrived = exchange(jnp.broadcast_to(sent[None], (n_grid,) + sent.shape))

    first = col_index == 0
    spec_all = jnp.concatenate(
        [jnp.where(first, spectrum, spectrum_other), jnp.where(first, spectrum_other, spectrum)], axis=0
    )
    grad_spec = weight_grad(where, back_terms, spec_all, own_chan, scale_inv)
    point_back = point_mixing(where, [grad_pre, pre_other], w_point, True)
    arrived, grad_spec, point_back = lax.optimization_barrier((arrived, grad_spec, point_back))

    grad_in = last(point_back, y_tab, x_tab, arrived, sizes)
    sums = sum_of_slabs(arrived[:, own_chan:], sums.shape)
    grad_point = sums[:, : 2 * own_chan]
    grad_bias = sums[:, 2 * own_chan : 2 * own_chan + NCLASS].T
    return (act_out, grad_in, grad_spec, grad_point, grad_bias)


def solution(mesh):
    return jax.shard_map(
        functools.partial(on_device, mesh.shape["gx"], mesh.shape["gy"]),
        mesh=mesh,
        in_specs=(
            P(("groups", "col"), "gx", "gy"),
            P(("groups", "gx"), "gy"),
            P(),
            P(),
            P(None, None, "col", "gx", "gy"),
            P(("groups", "col"), "gx", "gy"),
        ),
        out_specs=(
            P(("groups", "col"), "gx", "gy"),
            P(("groups", "col"), "gx", "gy"),
            P("groups", None, "col", "gx", "gy"),
            P(("groups", "col"), None),
            P("groups", "col"),
        ),
        check_vma=False,
    )
```

```python
import functools
import math

import jax
import jax.numpy as jnp
import numpy as np
from jax import lax
from jax.experimental import pallas as pl
from jax.experimental.pallas import tpu as pltpu
from jax.sharding import PartitionSpec as P

TILE = 16
NCLASS = 8
VMEM_BYTES = 48 * 1024 * 1024
SPLITS = 2

inv_root_two = 0.7071067811865476
inv_root_tau = 0.3989422804014327

f32 = jnp.float32
bf16 = jnp.bfloat16


def dot_nn(a, b):
    return lax.dot_general(a, b, (((1,), (0,)), ((), ())), preferred_element_type=f32)


def dot_nt(a, b):
    return lax.dot_general(a, b, (((1,), (1,)), ((), ())), preferred_element_type=f32)


def dot_tn(a, b):
    return lax.dot_general(a, b, (((0,), (0,)), ((), ())), preferred_element_type=f32)


def params(limit=VMEM_BYTES):
    return pltpu.CompilerParams(vmem_limit_bytes=limit)


def cost(flops, *arrays, transcendentals=0):
    size = sum(math.prod(a.shape) * jnp.dtype(a.dtype).itemsize for a in arrays)
    return pl.CostEstimate(flops=int(flops), bytes_accessed=int(size), transcendentals=int(transcendentals))


def divisor(length, limit):
    return max(d for d in range(1, limit + 1) if length % d == 0)


def y_table(n_y, m_y, offset, length):
    turns = (np.arange(m_y)[:, None] * np.arange(n_y)[None, :]) % n_y * (2.0 * math.pi / n_y)
    whole = np.concatenate([np.cos(turns), -np.sin(turns)]).astype(bf16)
    return lax.dynamic_slice_in_dim(jnp.asarray(whole), offset, length, 1)


def x_table(n_x, m_x, own_m, offset, length):
    freq = np.arange(m_x)
    signed = np.where(freq < m_x // 2, freq, freq - m_x)
    turns = (np.arange(n_x)[:, None] * signed[None, :]) % n_x * (2.0 * math.pi / n_x)
    cos_part = np.cos(turns).reshape(n_x, m_x // own_m, 1, own_m)
    sin_part = np.sin(turns).reshape(n_x, m_x // own_m, 1, own_m)
    real_row = np.concatenate([cos_part, -sin_part], axis=2).reshape(n_x, 2 * m_x)
    imag_row = np.concatenate([sin_part, cos_part], axis=2).reshape(n_x, 2 * m_x)
    whole = np.stack([real_row, imag_row]).astype(bf16)
    return lax.dynamic_slice_in_dim(jnp.asarray(whole), offset, length, 1)


def exchange(chunks):
    return lax.all_to_all(chunks, ("gx", "gy"), 0, 0, tiled=True)


def put_chunks(ref, channel, value, n_gy):
    own_k, lanes = ref.shape[2:]
    for place in range(ref.shape[0]):
        a, b = divmod(place, n_gy)
        piece = value[a * own_k : (a + 1) * own_k, b * lanes : (b + 1) * lanes]
        ref[place, channel] = piece.astype(bf16)


def take_chunks(ref, channel, n_gy):
    own_k, lanes = ref.shape[2:]
    kind = bf16 if own_k % 16 == 0 and lanes % 128 == 0 else f32
    rows = [
        jnp.concatenate([ref[a + b, channel].astype(kind) for b in range(n_gy)], axis=1)
        for a in range(0, ref.shape[0], n_gy)
    ]
    return jnp.concatenate(rows, axis=0).astype(bf16)


def rows_of_modes(modes, x_ref):
    return [dot_nt(x_ref[part], modes).astype(bf16) for part in range(2)]


def forward_kernel(n_gy, where_ref, state_ref, y_ref, x_ref, out_ref):
    half = y_ref.shape[0] // 2
    for c in range(state_ref.shape[0]):
        rows = dot_nt(y_ref[...], state_ref[c]).astype(bf16)
        terms = dot_nn(rows[:half], x_ref[0]) + dot_nn(rows[half:], x_ref[1])
        put_chunks(out_ref, c, terms, n_gy)


def over_channels(kernel, where, fields, tables, modes, out_specs, out_shape, steps, flops, name, limit, before=(), aliases=None):
    n_rows, n_cols = fields[0][0].shape[1:]
    y_tab, x_tab = tables
    table_specs = [
        pl.BlockSpec(y_tab.shape, lambda c, w: (0, 0)),
        pl.BlockSpec(x_tab.shape, lambda c, w: (0, 0, 0)),
    ]
    moved = [jax.ShapeDtypeStruct((steps,) + spec.block_shape, bf16) for _, spec in fields]
    return pl.pallas_call(
        kernel,
        grid_spec=pltpu.PrefetchScalarGridSpec(
            num_scalar_prefetch=1,
            grid=(steps,),
            in_specs=[spec for _, spec in fields]
            + table_specs
            + [spec for _, spec in modes]
            + [pl.BlockSpec(memory_space=pl.ANY)] * len(before),
            out_specs=out_specs,
        ),
        out_shape=out_shape,
        input_output_aliases=aliases or {},
        compiler_params=params(limit),
        cost_estimate=cost(flops, *moved, *moved),
        name=name,
    )(where, *[a for a, _ in fields], y_tab, x_tab, *[a for a, _ in modes], *before)


def transform_flops(shape, y_tab, x_tab):
    channels, n_rows, n_cols = shape
    return 2 * channels * n_rows * y_tab.shape[0] * (n_cols + x_tab.shape[2])


def forward_modes(where, state, tables, sizes, own_k):
    channels, n_rows, n_cols = state.shape
    out = jax.ShapeDtypeStruct((sizes[0] * sizes[1], channels, own_k, tables[1].shape[2] // sizes[1]), bf16)
    step = divisor(channels, 4)
    return over_channels(
        functools.partial(forward_kernel, sizes[1]),
        where,
        [(state, pl.BlockSpec((step, n_rows, n_cols), lambda c, w: (c, 0, 0)))],
        tables,
        [],
        pl.BlockSpec((out.shape[0], step) + out.shape[2:], lambda c, w: (0, c, 0, 0)),
        out,
        channels // step,
        transform_flops(state.shape, *tables),
        "forward_modes",
        VMEM_BYTES,
    )


def gelu_parts(v):
    v = v.astype(bf16)
    half = jnp.asarray(0.5, bf16)
    bell = jnp.exp2(v * v * jnp.asarray(-0.5 * math.log2(math.e), bf16)) * jnp.asarray(inv_root_tau, bf16)
    cdf = lax.erf(v * jnp.asarray(inv_root_two, bf16)).astype(bf16) * half + half
    return v * cdf, cdf + v * bell


def middle_kernel(n_gy, row_step, where_ref, mix_ref, out_grad_ref, y_ref, x_ref, mode_ref, *refs):
    act_ref, pre_ref, out_ref = refs[-3:]
    n_rows = mix_ref.shape[1]
    half = y_ref.shape[0] // 2
    for c in range(mix_ref.shape[0]):
        space = jnp.concatenate(rows_of_modes(take_chunks(mode_ref, c, n_gy), x_ref), axis=1)
        back = []
        for start in range(0, n_rows, row_step):
            rows = slice(start, start + row_step)
            v = dot_nn(space[rows], y_ref[...]) + mix_ref[c, rows].astype(f32)
            act, slope = gelu_parts(v)
            act_ref[c, rows] = act
            pre = out_grad_ref[c, rows] * slope
            pre_ref[c, rows] = pre
            back.append(dot_nt(pre, y_ref[...]).astype(bf16))
        back = jnp.concatenate(back, axis=0)
        terms = dot_tn(back[:, :half], x_ref[0]) + dot_tn(back[:, half:], x_ref[1])
        put_chunks(out_ref, c, terms, n_gy)


def middle(where, mix, out_grad, tables, modes, sizes, first=0, before=()):
    channels, n_rows, n_cols = mix.shape
    count = modes.shape[1]
    step = divisor(count, 2)
    skip = first // step
    field = pl.BlockSpec((step, n_rows, n_cols), lambda c, w: (c + skip, 0, 0))
    chunk = (modes.shape[0], step) + modes.shape[2:]
    chunks = jax.ShapeDtypeStruct((modes.shape[0], channels) + modes.shape[2:], bf16)
    return over_channels(
        functools.partial(middle_kernel, sizes[1], min(256, n_rows)),
        where,
        [(mix, field), (out_grad, field)],
        tables,
        [(modes, pl.BlockSpec(chunk, lambda c, w: (0, c, 0, 0)))],
        [field, field, pl.BlockSpec(chunk, lambda c, w: (0, c + skip, 0, 0))],
        [jax.ShapeDtypeStruct(mix.shape, bf16)] * 2 + [chunks],
        count // step,
        2 * transform_flops((count, n_rows, n_cols), *tables),
        "middle",
        VMEM_BYTES,
        before,
        {6 + n: n for n in range(len(before))},
    )


def last_kernel(n_gy, where_ref, point_ref, y_ref, x_ref, mode_ref, mark_ref, out_ref):
    for c in range(point_ref.shape[0]):
        space = jnp.concatenate(rows_of_modes(take_chunks(mode_ref, c, n_gy), x_ref), axis=1)
        out_ref[c] = (dot_nn(space, y_ref[...]) + point_ref[c].astype(f32)).astype(bf16)


def last(where, point_back, tables, modes, sizes, mark):
    channels, n_rows, n_cols = point_back.shape
    step = divisor(channels, 4)
    field = pl.BlockSpec((step, n_rows, n_cols), lambda c, w: (c, 0, 0))
    chunk = pl.BlockSpec((modes.shape[0], step) + modes.shape[2:], lambda c, w: (0, c, 0, 0))
    return over_channels(
        functools.partial(last_kernel, sizes[1]),
        where,
        [(point_back, field)],
        tables,
        [(modes, chunk)],
        field,
        jax.ShapeDtypeStruct(point_back.shape, bf16),
        channels // step,
        transform_flops(point_back.shape, *tables),
        "last",
        VMEM_BYTES,
        [mark],
    )


def chooser(rows, columns, first):
    channel = lax.broadcasted_iota(jnp.int32, (rows, columns), 0) // TILE + first
    return channel == lax.broadcasted_iota(jnp.int32, (rows, columns), 1)


def same_row(rows, columns):
    return lax.broadcasted_iota(jnp.int32, (rows, columns), 0) % TILE == (
        lax.broadcasted_iota(jnp.int32, (rows, columns), 1) % TILE
    )


def spread(weight, out_first, in_first, wide, transposed):
    channels = weight.shape[0]
    picks_out = chooser(wide, channels, out_first).astype(bf16)
    picks_in = chooser(wide, channels, in_first).astype(bf16)
    half = dot_nt(picks_out, weight) if transposed else dot_nn(picks_out, weight)
    return jnp.where(same_row(wide, wide), dot_nt(half.astype(bf16), picks_in), 0.0).astype(bf16)


def point_kernel(transposed, where_ref, own_ref, other_ref, weight_ref, *refs):
    bias_ref, (out_ref, mark_ref, spread_ref) = refs[:-3], refs[-3:]
    channels, n_rows, n_cols = out_ref.shape
    wide = channels * TILE

    @pl.when(pl.program_id(0) == 0)
    def _():
        own = where_ref[0] * channels
        for n, first in enumerate((own, channels - own)):
            spread_ref[n] = spread(weight_ref[...], own, first, wide, transposed)
        mark_ref[...] = jnp.zeros_like(mark_ref)

    for tile in range(n_rows // TILE):
        rows = slice(tile * TILE, (tile + 1) * TILE)
        total = dot_nn(spread_ref[0], own_ref[:, rows].reshape(wide, n_cols))
        total = total + dot_nn(spread_ref[1], other_ref[:, rows].reshape(wide, n_cols))
        total = total.reshape(channels, TILE, n_cols)
        for ref in bias_ref:
            total = total + ref[tile][:, None, :]
        out_ref[:, rows] = total.astype(bf16)


def over_rows(kernel, where, fields, others, other_specs, out_specs, out_shape, scratch, step, flops, name, limit):
    channels, n_rows, n_cols = fields[0].shape
    field = pl.BlockSpec((channels, step, n_cols), lambda r, w: (0, r, 0))
    outs = out_shape if isinstance(out_shape, list) else [out_shape]
    return pl.pallas_call(
        kernel,
        grid_spec=pltpu.PrefetchScalarGridSpec(
            num_scalar_prefetch=1,
            grid=(n_rows // step,),
            in_specs=[field] * len(fields) + other_specs,
            out_specs=out_specs,
            scratch_shapes=scratch,
        ),
        out_shape=out_shape,
        compiler_params=params(limit),
        cost_estimate=cost(flops, *fields, *others, *outs),
        name=name,
    )(where, *fields, *others)


def whole_spec(array):
    return pl.BlockSpec(array.shape, lambda r, w: (0,) * array.ndim)


def row_step(n_rows, limit):
    return TILE * divisor(n_rows // TILE, limit // TILE)


def point_mixing(where, fields, weight, transposed, bias=()):
    channels, n_rows, n_cols = fields[0].shape
    step = row_step(n_rows, 128)
    wide = channels * TILE
    return over_rows(
        functools.partial(point_kernel, transposed),
        where,
        fields,
        [weight, *bias],
        [whole_spec(weight)]
        + [pl.BlockSpec((step // TILE, channels, n_cols), lambda r, w: (r, 0, 0)) for _ in bias],
        [pl.BlockSpec((channels, step, n_cols), lambda r, w: (0, r, 0)), pl.BlockSpec((8, 128), lambda r, w: (0, 0))],
        [jax.ShapeDtypeStruct(fields[0].shape, bf16), jax.ShapeDtypeStruct((8, 128), f32)],
        [pltpu.VMEM((2, wide, wide), bf16)],
        step,
        4 * wide * wide * n_cols * (n_rows // TILE),
        "point_mixing",
        VMEM_BYTES,
    )


def sums_kernel(scale, where_ref, pre_ref, own_ref, other_ref, class_ref, out_ref, square_ref, bias_ref):
    channels, n_rows, n_cols = pre_ref.shape
    wide = channels * TILE
    step, last_step = pl.program_id(0), pl.num_programs(0) - 1

    @pl.when(step == 0)
    def _():
        square_ref[...] = jnp.zeros_like(square_ref)
        bias_ref[...] = jnp.zeros_like(bias_ref)

    for tile in range(n_rows // TILE):
        rows = slice(tile * TILE, (tile + 1) * TILE)
        pre = pre_ref[:, rows].reshape(wide, n_cols)
        square_ref[0] += dot_nt(pre, own_ref[:, rows].reshape(wide, n_cols))
        square_ref[1] += dot_nt(pre, other_ref[:, rows].reshape(wide, n_cols))
        bias_ref[...] += dot_nt(pre, class_ref[tile])

    @pl.when(step == last_step)
    def _():
        own = where_ref[0] * channels
        lanes = out_ref.shape[1]
        high = lax.Precision.HIGHEST
        total = jnp.zeros((wide, lanes), f32)
        for n, first in enumerate((own, channels - own)):
            kept = jnp.where(same_row(wide, wide), square_ref[n], 0.0)
            total = total + jnp.dot(kept, chooser(wide, lanes, first).astype(f32), precision=high)
        shift = lax.broadcasted_iota(jnp.int32, (NCLASS, lanes), 0) + 2 * channels
        shift = (shift == lax.broadcasted_iota(jnp.int32, (NCLASS, lanes), 1)).astype(f32)
        total = total + jnp.dot(bias_ref[...], shift, precision=high)
        out_ref[...] = total.reshape(channels, TILE, lanes).sum(axis=1) * scale


def cell_sums(where, pre, state_own, state_other, classes, scale):
    channels, n_rows, n_cols = pre.shape
    step = row_step(n_rows, 64)
    wide = channels * TILE
    return over_rows(
        functools.partial(sums_kernel, scale),
        where,
        [pre, state_own, state_other],
        [classes],
        [pl.BlockSpec((step // TILE, NCLASS, n_cols), lambda r, w: (r, 0, 0))],
        pl.BlockSpec((channels, 128), lambda r, w: (0, 0)),
        jax.ShapeDtypeStruct((channels, 128), f32),
        [pltpu.VMEM((2, wide, wide), f32), pltpu.VMEM((wide, NCLASS), f32)],
        step,
        4 * wide * wide * n_cols * (n_rows // TILE),
        "cell_sums",
        VMEM_BYTES,
    )


def mode_weight(where_ref, own_k, scale):
    k = where_ref[1] * own_k + lax.broadcasted_iota(jnp.int32, (own_k, 1), 0)
    return jnp.where(k == 0, scale, 2.0 * scale).astype(f32)


def times_i(value):
    half = value.shape[-1] // 2
    return jnp.concatenate([-value[..., half:], value[..., :half]], axis=-1)


def twice(value):
    return jnp.concatenate([value, value], axis=-1)


def mix_kernel(scale, where_ref, weight_ref, own_ref, other_ref, out_ref, spec_ref, turned_ref):
    channels, own_k, lanes = own_ref.shape

    @pl.when(pl.program_id(0) == 0)
    def _():
        own = where_ref[0] * channels
        for source, first in ((own_ref, own), (other_ref, channels - own)):
            for c in range(channels):
                spec_ref[first + c] = source[c]
                turned_ref[first + c] = times_i(source[c])

    factor = mode_weight(where_ref, own_k, scale)
    for o in range(weight_ref.shape[2]):
        total = jnp.zeros((own_k, lanes), f32)
        for i in range(2 * channels):
            w_real, w_imag = twice(weight_ref[0, i, o]), twice(weight_ref[1, i, o])
            total = total + (w_real * spec_ref[i] + w_imag * turned_ref[i]).astype(f32)
        value = (total * factor).astype(bf16)
        for place in range(out_ref.shape[0]):
            out_ref[place, o] = value


def mix_modes(where, weights, own, other, copies, scale, first, count):
    n_in, n_out, own_k, own_m = weights.shape[1:]
    lanes = 2 * own_m
    step = divisor(count, 4)
    skip = first // step
    spec = pl.BlockSpec(own.shape, lambda o, w: (0, 0, 0))
    weight = pl.BlockSpec((2, n_in, step, own_k, own_m), lambda o, w: (0, 0, o + skip, 0, 0))
    return pl.pallas_call(
        functools.partial(mix_kernel, scale),
        grid_spec=pltpu.PrefetchScalarGridSpec(
            num_scalar_prefetch=1,
            grid=(count // step,),
            in_specs=[weight, spec, spec],
            out_specs=pl.BlockSpec((copies, step, own_k, lanes), lambda o, w: (0, o, 0, 0)),
            scratch_shapes=[pltpu.VMEM((n_in, own_k, lanes), bf16)] * 2,
        ),
        out_shape=jax.ShapeDtypeStruct((copies, count, own_k, lanes), bf16),
        compiler_params=params(),
        cost_estimate=cost(4 * n_in * count * own_k * lanes, weights),
        name="mix_modes",
    )(where, weights, own, other)


def sum_chunks(where_ref, chunk_refs, scale):
    own_k = chunk_refs[0].shape[2]
    factor = mode_weight(where_ref, own_k, scale)
    for ref in chunk_refs:
        for channel in range(ref.shape[1]):
            total = ref[0, channel].astype(f32)
            for place in range(1, ref.shape[0]):
                total = total + ref[place, channel].astype(f32)
            yield total * factor


def back_kernel(scale, scale_out, n_chunks, where_ref, weight_ref, *refs):
    out_ref, grad_ref, turned_ref = refs[n_chunks:]

    @pl.when(pl.program_id(0) == 0)
    def _():
        for o, value in enumerate(sum_chunks(where_ref, refs[:n_chunks], scale)):
            grad_ref[o] = value.astype(bf16)
            turned_ref[o] = times_i(value).astype(bf16)

    for i in range(weight_ref.shape[1]):
        total = jnp.zeros(out_ref.shape[1:], f32)
        for o in range(weight_ref.shape[2]):
            w_real, w_imag = twice(weight_ref[0, i, o]), twice(weight_ref[1, i, o])
            total = total + (w_real * grad_ref[o] - w_imag * turned_ref[o]).astype(f32)
        out_ref[i] = total * scale_out


def back_mix(where, weights, chunks, scale, scale_out):
    n_in, n_out, own_k, own_m = weights.shape[1:]
    lanes = 2 * own_m
    step = divisor(n_in // 2, 8)
    blocks = n_in // step
    half = blocks // 2
    weight = pl.BlockSpec(
        (2, step, n_out, own_k, own_m), lambda i, w: (0, (i + (1 - w[0]) * half) % blocks, 0, 0, 0)
    )
    return pl.pallas_call(
        functools.partial(back_kernel, scale, scale_out, len(chunks)),
        grid_spec=pltpu.PrefetchScalarGridSpec(
            num_scalar_prefetch=1,
            grid=(blocks,),
            in_specs=[weight] + [pl.BlockSpec(c.shape, lambda i, w: (0, 0, 0, 0)) for c in chunks],
            out_specs=pl.BlockSpec((step, own_k, lanes), lambda i, w: (i, 0, 0)),
            scratch_shapes=[pltpu.VMEM((n_out, own_k, lanes), bf16)] * 2,
        ),
        out_shape=jax.ShapeDtypeStruct((n_in, own_k, lanes), f32),
        compiler_params=params(),
        cost_estimate=cost(4 * n_in * n_out * own_k * lanes, weights),
        name="back_mix",
    )(where, weights, *chunks)


def weight_kernel(scale, n_chunks, where_ref, spec_ref, *refs):
    out_ref, real_ref, imag_ref = refs[n_chunks:]
    n_out, own_k, own_m = real_ref.shape

    @pl.when(pl.program_id(0) == 0)
    def _():
        for o, value in enumerate(sum_chunks(where_ref, refs[:n_chunks], scale)):
            real_ref[o] = value[:, :own_m]
            imag_ref[o] = value[:, own_m:]

    for i in range(out_ref.shape[1]):
        value = spec_ref[i].astype(f32)
        s_real, s_imag = value[:, :own_m], value[:, own_m:]
        for o in range(n_out):
            g_real, g_imag = real_ref[o], imag_ref[o]
            out_ref[0, i, o] = g_real * s_real + g_imag * s_imag
            out_ref[1, i, o] = g_imag * s_real - g_real * s_imag


def weight_grad(where, chunks, spec_all, n_out, scale):
    n_in, own_k, lanes = spec_all.shape
    own_m = lanes // 2
    step = divisor(n_in, 4)
    out = jax.ShapeDtypeStruct((2, n_in, n_out, own_k, own_m), f32)
    return pl.pallas_call(
        functools.partial(weight_kernel, scale, len(chunks)),
        grid_spec=pltpu.PrefetchScalarGridSpec(
            num_scalar_prefetch=1,
            grid=(n_in // step,),
            in_specs=[pl.BlockSpec((step, own_k, lanes), lambda i, w: (i, 0, 0))]
            + [pl.BlockSpec(c.shape, lambda i, w: (0, 0, 0, 0)) for c in chunks],
            out_specs=pl.BlockSpec((2, step, n_out, own_k, own_m), lambda i, w: (0, i, 0, 0, 0)),
            scratch_shapes=[pltpu.VMEM((n_out, own_k, own_m), f32)] * 2,
        ),
        out_shape=out,
        compiler_params=params(),
        cost_estimate=cost(6 * n_in * n_out * own_k * own_m, out, out),
        name="weight_grad",
    )(where, spec_all, *chunks)


def slabs_of(value, shape):
    high = lax.reduce_precision(value, 8, 7)
    parts = jnp.stack([high, value - high]).astype(bf16).reshape(-1)
    size = math.prod(shape)
    count = -(-parts.shape[0] // size)
    return jnp.pad(parts, (0, count * size - parts.shape[0])).reshape((count,) + shape)


def sum_of_slabs(slabs, shape):
    total = slabs.astype(f32).sum(axis=0).reshape(-1)
    return total[: 2 * math.prod(shape)].reshape((2,) + shape).sum(axis=0)


def on_device(n_gx, n_gy, state_in, tile_class, class_bias, w_point, spec_weight, grad_out):
    sizes = (n_gx, n_gy)
    n_grid = n_gx * n_gy
    own_chan, n_rows, n_cols = state_in.shape
    own_k, own_m = spec_weight.shape[3:]
    m_y, m_x = own_k * n_gx, own_m * n_gy
    n_x, n_y = n_rows * n_gx, n_cols * n_gy
    gx_index = lax.axis_index("gx")
    gy_index = lax.axis_index("gy")
    col_index = lax.axis_index("col")
    scale_fwd = 1.0 / math.sqrt(n_x * n_y)
    scale_inv = 1.0 / math.sqrt(2.0 * m_x * m_y)
    other = [(0, 1), (1, 0)]
    where = jnp.stack([col_index, gx_index]).astype(jnp.int32)

    state_other = lax.ppermute(state_in, "col", other)
    y_tab = y_table(n_y, m_y, gy_index * n_cols, n_cols)
    x_tab = x_table(n_x, m_x, own_m, gx_index * n_rows, n_rows)
    tables = (y_tab, x_tab)

    tile_rows, tile_cols = tile_class.shape
    one_hot = (tile_class[:, None, :] == jnp.arange(NCLASS, dtype=jnp.int32)[None, :, None]).astype(f32)
    widen = jnp.asarray(np.repeat(np.eye(tile_cols), TILE, axis=1).astype(np.float32))
    bias_own = lax.dynamic_slice_in_dim(class_bias, col_index * own_chan, own_chan, 1)
    tile_bias = jnp.sum(one_hot[:, :, None, :] * bias_own[None, :, :, None], axis=1)
    bias = jnp.dot(
        tile_bias.reshape(tile_rows * own_chan, tile_cols), widen, precision=lax.Precision.HIGHEST
    ).reshape(tile_rows, own_chan, n_cols)
    classes = jnp.dot(
        one_hot.astype(bf16).reshape(tile_rows * NCLASS, tile_cols), widen.astype(bf16), preferred_element_type=f32
    )
    classes = classes.astype(bf16).reshape(tile_rows, NCLASS, n_cols)
    mix, _ = point_mixing(where, [state_in, state_other], w_point, False, [bias])

    terms = exchange(forward_modes(where, state_in, tables, sizes, own_k))
    terms, mix = lax.optimization_barrier((terms, mix))
    spectrum = (terms.astype(f32).sum(axis=0) * scale_fwd).astype(bf16)
    spectrum_other = lax.ppermute(spectrum, "col", other)
    halves = SPLITS if own_chan % SPLITS == 0 else 1
    count = own_chan // halves
    mixed = [
        exchange(
            mix_modes(where, spec_weight, spectrum, spectrum_other, n_grid, scale_inv, n * count, count)
        )
        for n in range(halves)
    ]

    done = ()
    for n in range(halves):
        done = middle(where, mix, grad_out, tables, mixed[n], sizes, n * count, done)
    act_out, grad_pre, back_terms = done
    back_terms = [exchange(back_terms)]
    pre_other = lax.ppermute(grad_pre, "col", other)

    sums = cell_sums(where, grad_pre, state_in, state_other, classes, scale_fwd)
    sums, *back_terms = lax.optimization_barrier((sums, *back_terms))

    input_terms = back_mix(where, spec_weight, back_terms, scale_inv, scale_fwd)
    input_modes = input_terms[own_chan:] + lax.ppermute(input_terms[:own_chan], "col", other)
    sent = jnp.concatenate([input_modes.astype(bf16), slabs_of(sums, input_modes.shape[1:])], axis=0)
    arrived = exchange(jnp.broadcast_to(sent[None], (n_grid,) + sent.shape))

    first = col_index == 0
    spec_all = jnp.concatenate(
        [jnp.where(first, spectrum, spectrum_other), jnp.where(first, spectrum_other, spectrum)], axis=0
    )
    grad_spec = weight_grad(where, back_terms, spec_all, own_chan, scale_inv)
    point_back, mark = point_mixing(where, [grad_pre, pre_other], w_point, True)
    arrived, grad_spec, mark = lax.optimization_barrier((arrived, grad_spec, mark))

    grad_in = last(where, point_back, tables, arrived, sizes, mark)
    sums = sum_of_slabs(arrived[:, own_chan:], sums.shape)
    grad_point = sums[:, : 2 * own_chan]
    grad_bias = sums[:, 2 * own_chan : 2 * own_chan + NCLASS].T
    return (act_out, grad_in, grad_spec, grad_point, grad_bias)


def solution(mesh):
    return jax.shard_map(
        functools.partial(on_device, mesh.shape["gx"], mesh.shape["gy"]),
        mesh=mesh,
        in_specs=(
            P(("groups", "col"), "gx", "gy"),
            P(("groups", "gx"), "gy"),
            P(),
            P(),
            P(None, None, "col", "gx", "gy"),
            P(("groups", "col"), "gx", "gy"),
        ),
        out_specs=(
            P(("groups", "col"), "gx", "gy"),
            P(("groups", "col"), "gx", "gy"),
            P("groups", None, "col", "gx", "gy"),
            P(("groups", "col"), None),
            P("groups", "col"),
        ),
        check_vma=False,
    )
```

```python
import functools
import math

import jax
import jax.numpy as jnp
import numpy as np
from jax import lax
from jax.experimental import pallas as pl
from jax.experimental.pallas import tpu as pltpu
from jax.sharding import PartitionSpec as P

TILE = 16
NCLASS = 8
VMEM_BYTES = 48 * 1024 * 1024
SPLITS = 2

inv_root_two = 0.7071067811865476
inv_root_tau = 0.3989422804014327

f32 = jnp.float32
bf16 = jnp.bfloat16


def dot_nn(a, b):
    return lax.dot_general(a, b, (((1,), (0,)), ((), ())), preferred_element_type=f32)


def dot_nt(a, b):
    return lax.dot_general(a, b, (((1,), (1,)), ((), ())), preferred_element_type=f32)


def dot_tn(a, b):
    return lax.dot_general(a, b, (((0,), (0,)), ((), ())), preferred_element_type=f32)


def params(limit=VMEM_BYTES):
    return pltpu.CompilerParams(vmem_limit_bytes=limit)


def cost(flops, *arrays, transcendentals=0):
    size = sum(math.prod(a.shape) * jnp.dtype(a.dtype).itemsize for a in arrays)
    return pl.CostEstimate(flops=int(flops), bytes_accessed=int(size), transcendentals=int(transcendentals))


def divisor(length, limit):
    return max(d for d in range(1, limit + 1) if length % d == 0)


def y_table(n_y, m_y, offset, length):
    turns = (np.arange(m_y)[:, None] * np.arange(n_y)[None, :]) % n_y * (2.0 * math.pi / n_y)
    whole = np.concatenate([np.cos(turns), -np.sin(turns)]).astype(bf16)
    return lax.dynamic_slice_in_dim(jnp.asarray(whole), offset, length, 1)


def x_table(n_x, m_x, own_m, offset, length):
    freq = np.arange(m_x)
    signed = np.where(freq < m_x // 2, freq, freq - m_x)
    turns = (np.arange(n_x)[:, None] * signed[None, :]) % n_x * (2.0 * math.pi / n_x)
    cos_part = np.cos(turns).reshape(n_x, m_x // own_m, 1, own_m)
    sin_part = np.sin(turns).reshape(n_x, m_x // own_m, 1, own_m)
    real_row = np.concatenate([cos_part, -sin_part], axis=2).reshape(n_x, 2 * m_x)
    imag_row = np.concatenate([sin_part, cos_part], axis=2).reshape(n_x, 2 * m_x)
    whole = np.stack([real_row, imag_row]).astype(bf16)
    return lax.dynamic_slice_in_dim(jnp.asarray(whole), offset, length, 1)


def exchange(chunks):
    return lax.all_to_all(chunks, ("gx", "gy"), 0, 0, tiled=True)


def put_chunks(ref, channel, value, n_gy):
    own_k, lanes = ref.shape[2:]
    for place in range(ref.shape[0]):
        a, b = divmod(place, n_gy)
        piece = value[a * own_k : (a + 1) * own_k, b * lanes : (b + 1) * lanes]
        ref[place, channel] = piece.astype(bf16)


def take_chunks(ref, channel, n_gy):
    own_k, lanes = ref.shape[2:]
    kind = bf16 if own_k % 16 == 0 and lanes % 128 == 0 else f32
    rows = [
        jnp.concatenate([ref[a + b, channel].astype(kind) for b in range(n_gy)], axis=1)
        for a in range(0, ref.shape[0], n_gy)
    ]
    return jnp.concatenate(rows, axis=0).astype(bf16)


def rows_of_modes(modes, x_ref):
    return [dot_nt(x_ref[part], modes).astype(bf16) for part in range(2)]


def forward_kernel(n_gy, where_ref, state_ref, y_ref, x_ref, out_ref):
    half = y_ref.shape[0] // 2
    for c in range(state_ref.shape[0]):
        rows = dot_nt(y_ref[...], state_ref[c]).astype(bf16)
        terms = dot_nn(rows[:half], x_ref[0]) + dot_nn(rows[half:], x_ref[1])
        put_chunks(out_ref, c, terms, n_gy)


def over_channels(kernel, where, fields, tables, modes, out_specs, out_shape, steps, flops, name, limit, before=(), aliases=None):
    n_rows, n_cols = fields[0][0].shape[1:]
    y_tab, x_tab = tables
    table_specs = [
        pl.BlockSpec(y_tab.shape, lambda c, w: (0, 0)),
        pl.BlockSpec(x_tab.shape, lambda c, w: (0, 0, 0)),
    ]
    moved = [jax.ShapeDtypeStruct((steps,) + spec.block_shape, bf16) for _, spec in fields]
    return pl.pallas_call(
        kernel,
        grid_spec=pltpu.PrefetchScalarGridSpec(
            num_scalar_prefetch=1,
            grid=(steps,),
            in_specs=[spec for _, spec in fields]
            + table_specs
            + [spec for _, spec in modes]
            + [pl.BlockSpec(memory_space=pl.ANY)] * len(before),
            out_specs=out_specs,
        ),
        out_shape=out_shape,
        input_output_aliases=aliases or {},
        compiler_params=params(limit),
        cost_estimate=cost(flops, *moved, *moved),
        name=name,
    )(where, *[a for a, _ in fields], y_tab, x_tab, *[a for a, _ in modes], *before)


def transform_flops(shape, y_tab, x_tab):
    channels, n_rows, n_cols = shape
    return 2 * channels * n_rows * y_tab.shape[0] * (n_cols + x_tab.shape[2])


def forward_modes(where, state, tables, sizes, own_k):
    channels, n_rows, n_cols = state.shape
    out = jax.ShapeDtypeStruct((sizes[0] * sizes[1], channels, own_k, tables[1].shape[2] // sizes[1]), bf16)
    step = divisor(channels, 4)
    return over_channels(
        functools.partial(forward_kernel, sizes[1]),
        where,
        [(state, pl.BlockSpec((step, n_rows, n_cols), lambda c, w: (c, 0, 0)))],
        tables,
        [],
        pl.BlockSpec((out.shape[0], step) + out.shape[2:], lambda c, w: (0, c, 0, 0)),
        out,
        channels // step,
        transform_flops(state.shape, *tables),
        "forward_modes",
        VMEM_BYTES,
    )


def gelu_parts(v):
    v = v.astype(bf16)
    half = jnp.asarray(0.5, bf16)
    bell = jnp.exp2(v * v * jnp.asarray(-0.5 * math.log2(math.e), bf16)) * jnp.asarray(inv_root_tau, bf16)
    cdf = lax.erf(v * jnp.asarray(inv_root_two, bf16)).astype(bf16) * half + half
    return v * cdf, cdf + v * bell


def middle_kernel(n_gy, row_step, where_ref, mix_ref, out_grad_ref, y_ref, x_ref, mode_ref, *refs):
    act_ref, pre_ref, out_ref = refs[-3:]
    n_rows = mix_ref.shape[1]
    half = y_ref.shape[0] // 2
    for c in range(mix_ref.shape[0]):
        space = jnp.concatenate(rows_of_modes(take_chunks(mode_ref, c, n_gy), x_ref), axis=1)
        back = []
        for start in range(0, n_rows, row_step):
            rows = slice(start, start + row_step)
            v = dot_nn(space[rows], y_ref[...]) + mix_ref[c, rows].astype(f32)
            act, slope = gelu_parts(v)
            act_ref[c, rows] = act
            pre = out_grad_ref[c, rows] * slope
            pre_ref[c, rows] = pre
            back.append(dot_nt(pre, y_ref[...]).astype(bf16))
        back = jnp.concatenate(back, axis=0)
        terms = dot_tn(back[:, :half], x_ref[0]) + dot_tn(back[:, half:], x_ref[1])
        put_chunks(out_ref, c, terms, n_gy)


def middle(where, mix, out_grad, tables, modes, sizes, first=0, before=()):
    channels, n_rows, n_cols = mix.shape
    count = modes.shape[1]
    step = divisor(count, 2)
    skip = first // step
    field = pl.BlockSpec((step, n_rows, n_cols), lambda c, w: (c + skip, 0, 0))
    chunk = (modes.shape[0], step) + modes.shape[2:]
    chunks = jax.ShapeDtypeStruct((modes.shape[0], channels) + modes.shape[2:], bf16)
    return over_channels(
        functools.partial(middle_kernel, sizes[1], min(256, n_rows)),
        where,
        [(mix, field), (out_grad, field)],
        tables,
        [(modes, pl.BlockSpec(chunk, lambda c, w: (0, c, 0, 0)))],
        [field, field, pl.BlockSpec(chunk, lambda c, w: (0, c + skip, 0, 0))],
        [jax.ShapeDtypeStruct(mix.shape, bf16)] * 2 + [chunks],
        count // step,
        2 * transform_flops((count, n_rows, n_cols), *tables),
        "middle",
        VMEM_BYTES,
        before,
        {6 + n: n for n in range(len(before))},
    )


def last_kernel(n_gy, where_ref, point_ref, y_ref, x_ref, mode_ref, mark_ref, out_ref):
    for c in range(point_ref.shape[0]):
        space = jnp.concatenate(rows_of_modes(take_chunks(mode_ref, c, n_gy), x_ref), axis=1)
        out_ref[c] = (dot_nn(space, y_ref[...]) + point_ref[c].astype(f32)).astype(bf16)


def last(where, point_back, tables, modes, sizes, mark):
    channels, n_rows, n_cols = point_back.shape
    step = divisor(channels, 4)
    field = pl.BlockSpec((step, n_rows, n_cols), lambda c, w: (c, 0, 0))
    chunk = pl.BlockSpec((modes.shape[0], step) + modes.shape[2:], lambda c, w: (0, c, 0, 0))
    return over_channels(
        functools.partial(last_kernel, sizes[1]),
        where,
        [(point_back, field)],
        tables,
        [(modes, chunk)],
        field,
        jax.ShapeDtypeStruct(point_back.shape, bf16),
        channels // step,
        transform_flops(point_back.shape, *tables),
        "last",
        VMEM_BYTES,
        [mark],
    )


def chooser(rows, columns, first):
    channel = lax.broadcasted_iota(jnp.int32, (rows, columns), 0) // TILE + first
    return channel == lax.broadcasted_iota(jnp.int32, (rows, columns), 1)


def same_row(rows, columns):
    return lax.broadcasted_iota(jnp.int32, (rows, columns), 0) % TILE == (
        lax.broadcasted_iota(jnp.int32, (rows, columns), 1) % TILE
    )


def spread(weight, out_first, in_first, wide, transposed):
    channels = weight.shape[0]
    picks_out = chooser(wide, channels, out_first).astype(bf16)
    picks_in = chooser(wide, channels, in_first).astype(bf16)
    half = dot_nt(picks_out, weight) if transposed else dot_nn(picks_out, weight)
    return jnp.where(same_row(wide, wide), dot_nt(half.astype(bf16), picks_in), 0.0).astype(bf16)


def point_kernel(transposed, where_ref, own_ref, other_ref, weight_ref, *refs):
    bias_ref, (out_ref, mark_ref, spread_ref) = refs[:-3], refs[-3:]
    channels, n_rows, n_cols = out_ref.shape
    wide = channels * TILE

    @pl.when(pl.program_id(0) == 0)
    def _():
        own = where_ref[0] * channels
        for n, first in enumerate((own, channels - own)):
            spread_ref[n] = spread(weight_ref[...], own, first, wide, transposed)
        mark_ref[...] = jnp.zeros_like(mark_ref)

    for tile in range(n_rows // TILE):
        rows = slice(tile * TILE, (tile + 1) * TILE)
        total = dot_nn(spread_ref[0], own_ref[:, rows].reshape(wide, n_cols))
        total = total + dot_nn(spread_ref[1], other_ref[:, rows].reshape(wide, n_cols))
        total = total.reshape(channels, TILE, n_cols)
        for ref in bias_ref:
            total = total + ref[tile][:, None, :]
        out_ref[:, rows] = total.astype(bf16)


def over_rows(kernel, where, fields, others, other_specs, out_specs, out_shape, scratch, step, flops, name, limit):
    channels, n_rows, n_cols = fields[0].shape
    field = pl.BlockSpec((channels, step, n_cols), lambda r, w: (0, r, 0))
    outs = out_shape if isinstance(out_shape, list) else [out_shape]
    return pl.pallas_call(
        kernel,
        grid_spec=pltpu.PrefetchScalarGridSpec(
            num_scalar_prefetch=1,
            grid=(n_rows // step,),
            in_specs=[field] * len(fields) + other_specs,
            out_specs=out_specs,
            scratch_shapes=scratch,
        ),
        out_shape=out_shape,
        compiler_params=params(limit),
        cost_estimate=cost(flops, *fields, *others, *outs),
        name=name,
    )(where, *fields, *others)


def whole_spec(array):
    return pl.BlockSpec(array.shape, lambda r, w: (0,) * array.ndim)


def row_step(n_rows, limit):
    return TILE * divisor(n_rows // TILE, limit // TILE)


def point_mixing(where, fields, weight, transposed, bias=()):
    channels, n_rows, n_cols = fields[0].shape
    step = row_step(n_rows, 128)
    wide = channels * TILE
    return over_rows(
        functools.partial(point_kernel, transposed),
        where,
        fields,
        [weight, *bias],
        [whole_spec(weight)]
        + [pl.BlockSpec((step // TILE, channels, n_cols), lambda r, w: (r, 0, 0)) for _ in bias],
        [pl.BlockSpec((channels, step, n_cols), lambda r, w: (0, r, 0)), pl.BlockSpec((8, 128), lambda r, w: (0, 0))],
        [jax.ShapeDtypeStruct(fields[0].shape, bf16), jax.ShapeDtypeStruct((8, 128), f32)],
        [pltpu.VMEM((2, wide, wide), bf16)],
        step,
        4 * wide * wide * n_cols * (n_rows // TILE),
        "point_mixing",
        VMEM_BYTES,
    )


def sums_kernel(scale, where_ref, pre_ref, own_ref, other_ref, class_ref, out_ref, square_ref, bias_ref):
    channels, n_rows, n_cols = pre_ref.shape
    wide = channels * TILE
    step, last_step = pl.program_id(0), pl.num_programs(0) - 1

    @pl.when(step == 0)
    def _():
        square_ref[...] = jnp.zeros_like(square_ref)
        bias_ref[...] = jnp.zeros_like(bias_ref)

    for tile in range(n_rows // TILE):
        rows = slice(tile * TILE, (tile + 1) * TILE)
        pre = pre_ref[:, rows].reshape(wide, n_cols)
        square_ref[0] += dot_nt(pre, own_ref[:, rows].reshape(wide, n_cols))
        square_ref[1] += dot_nt(pre, other_ref[:, rows].reshape(wide, n_cols))
        bias_ref[...] += dot_nt(pre, class_ref[tile])

    @pl.when(step == last_step)
    def _():
        own = where_ref[0] * channels
        lanes = out_ref.shape[1]
        high = lax.Precision.HIGHEST
        total = jnp.zeros((wide, lanes), f32)
        for n, first in enumerate((own, channels - own)):
            kept = jnp.where(same_row(wide, wide), square_ref[n], 0.0)
            total = total + jnp.dot(kept, chooser(wide, lanes, first).astype(f32), precision=high)
        shift = lax.broadcasted_iota(jnp.int32, (NCLASS, lanes), 0) + 2 * channels
        shift = (shift == lax.broadcasted_iota(jnp.int32, (NCLASS, lanes), 1)).astype(f32)
        total = total + jnp.dot(bias_ref[...], shift, precision=high)
        out_ref[...] = total.reshape(channels, TILE, lanes).sum(axis=1) * scale


def cell_sums(where, pre, state_own, state_other, classes, scale):
    channels, n_rows, n_cols = pre.shape
    step = row_step(n_rows, 64)
    wide = channels * TILE
    return over_rows(
        functools.partial(sums_kernel, scale),
        where,
        [pre, state_own, state_other],
        [classes],
        [pl.BlockSpec((step // TILE, NCLASS, n_cols), lambda r, w: (r, 0, 0))],
        pl.BlockSpec((channels, 128), lambda r, w: (0, 0)),
        jax.ShapeDtypeStruct((channels, 128), f32),
        [pltpu.VMEM((2, wide, wide), f32), pltpu.VMEM((wide, NCLASS), f32)],
        step,
        4 * wide * wide * n_cols * (n_rows // TILE),
        "cell_sums",
        VMEM_BYTES,
    )


def mode_weight(where_ref, own_k, scale):
    k = where_ref[1] * own_k + lax.broadcasted_iota(jnp.int32, (own_k, 1), 0)
    return jnp.where(k == 0, scale, 2.0 * scale).astype(f32)


def times_i(value):
    half = value.shape[-1] // 2
    return jnp.concatenate([-value[..., half:], value[..., :half]], axis=-1)


def twice(value):
    return jnp.concatenate([value, value], axis=-1)


def mix_kernel(scale, where_ref, weight_ref, own_ref, other_ref, out_ref, spec_ref, turned_ref):
    channels, own_k, lanes = own_ref.shape

    @pl.when(pl.program_id(0) == 0)
    def _():
        own = where_ref[0] * channels
        for source, first in ((own_ref, own), (other_ref, channels - own)):
            for c in range(channels):
                spec_ref[first + c] = source[c]
                turned_ref[first + c] = times_i(source[c])

    factor = mode_weight(where_ref, own_k, scale)
    for o in range(weight_ref.shape[2]):
        total = jnp.zeros((own_k, lanes), f32)
        for i in range(2 * channels):
            w_real, w_imag = twice(weight_ref[0, i, o]), twice(weight_ref[1, i, o])
            total = total + (w_real * spec_ref[i] + w_imag * turned_ref[i]).astype(f32)
        value = (total * factor).astype(bf16)
        for place in range(out_ref.shape[0]):
            out_ref[place, o] = value


def mix_modes(where, weights, own, other, copies, scale, first, count):
    n_in, n_out, own_k, own_m = weights.shape[1:]
    lanes = 2 * own_m
    step = divisor(count, 4)
    skip = first // step
    spec = pl.BlockSpec(own.shape, lambda o, w: (0, 0, 0))
    weight = pl.BlockSpec((2, n_in, step, own_k, own_m), lambda o, w: (0, 0, o + skip, 0, 0))
    return pl.pallas_call(
        functools.partial(mix_kernel, scale),
        grid_spec=pltpu.PrefetchScalarGridSpec(
            num_scalar_prefetch=1,
            grid=(count // step,),
            in_specs=[weight, spec, spec],
            out_specs=pl.BlockSpec((copies, step, own_k, lanes), lambda o, w: (0, o, 0, 0)),
            scratch_shapes=[pltpu.VMEM((n_in, own_k, lanes), bf16)] * 2,
        ),
        out_shape=jax.ShapeDtypeStruct((copies, count, own_k, lanes), bf16),
        compiler_params=params(),
        cost_estimate=cost(4 * n_in * count * own_k * lanes, weights),
        name="mix_modes",
    )(where, weights, own, other)


def sum_chunks(where_ref, chunk_refs, scale):
    own_k = chunk_refs[0].shape[2]
    factor = mode_weight(where_ref, own_k, scale)
    for ref in chunk_refs:
        for channel in range(ref.shape[1]):
            total = ref[0, channel].astype(f32)
            for place in range(1, ref.shape[0]):
                total = total + ref[place, channel].astype(f32)
            yield total * factor


def back_kernel(scale, scale_out, n_chunks, where_ref, weight_ref, *refs):
    out_ref, grad_ref, turned_ref = refs[n_chunks:]

    @pl.when(pl.program_id(0) == 0)
    def _():
        for o, value in enumerate(sum_chunks(where_ref, refs[:n_chunks], scale)):
            grad_ref[o] = value.astype(bf16)
            turned_ref[o] = times_i(value).astype(bf16)

    for i in range(weight_ref.shape[1]):
        total = jnp.zeros(out_ref.shape[1:], f32)
        for o in range(weight_ref.shape[2]):
            w_real, w_imag = twice(weight_ref[0, i, o]), twice(weight_ref[1, i, o])
            total = total + (w_real * grad_ref[o] - w_imag * turned_ref[o]).astype(f32)
        out_ref[i] = total * scale_out


def back_mix(where, weights, chunks, scale, scale_out):
    n_in, n_out, own_k, own_m = weights.shape[1:]
    lanes = 2 * own_m
    step = divisor(n_in // 2, 8)
    blocks = n_in // step
    half = blocks // 2
    weight = pl.BlockSpec(
        (2, step, n_out, own_k, own_m), lambda i, w: (0, (i + (1 - w[0]) * half) % blocks, 0, 0, 0)
    )
    return pl.pallas_call(
        functools.partial(back_kernel, scale, scale_out, len(chunks)),
        grid_spec=pltpu.PrefetchScalarGridSpec(
            num_scalar_prefetch=1,
            grid=(blocks,),
            in_specs=[weight] + [pl.BlockSpec(c.shape, lambda i, w: (0, 0, 0, 0)) for c in chunks],
            out_specs=pl.BlockSpec((step, own_k, lanes), lambda i, w: (i, 0, 0)),
            scratch_shapes=[pltpu.VMEM((n_out, own_k, lanes), bf16)] * 2,
        ),
        out_shape=jax.ShapeDtypeStruct((n_in, own_k, lanes), f32),
        compiler_params=params(),
        cost_estimate=cost(4 * n_in * n_out * own_k * lanes, weights),
        name="back_mix",
    )(where, weights, *chunks)


def weight_kernel(scale, n_chunks, where_ref, spec_ref, *refs):
    out_ref, real_ref, imag_ref = refs[n_chunks:]
    n_out, own_k, own_m = real_ref.shape

    @pl.when(pl.program_id(0) == 0)
    def _():
        for o, value in enumerate(sum_chunks(where_ref, refs[:n_chunks], scale)):
            real_ref[o] = value[:, :own_m]
            imag_ref[o] = value[:, own_m:]

    for i in range(out_ref.shape[1]):
        value = spec_ref[i].astype(f32)
        s_real, s_imag = value[:, :own_m], value[:, own_m:]
        for o in range(n_out):
            g_real, g_imag = real_ref[o], imag_ref[o]
            out_ref[0, i, o] = g_real * s_real + g_imag * s_imag
            out_ref[1, i, o] = g_imag * s_real - g_real * s_imag


def weight_grad(where, chunks, spec_all, n_out, scale):
    n_in, own_k, lanes = spec_all.shape
    own_m = lanes // 2
    step = divisor(n_in, 8)
    out = jax.ShapeDtypeStruct((2, n_in, n_out, own_k, own_m), f32)
    return pl.pallas_call(
        functools.partial(weight_kernel, scale, len(chunks)),
        grid_spec=pltpu.PrefetchScalarGridSpec(
            num_scalar_prefetch=1,
            grid=(n_in // step,),
            in_specs=[pl.BlockSpec((step, own_k, lanes), lambda i, w: (i, 0, 0))]
            + [pl.BlockSpec(c.shape, lambda i, w: (0, 0, 0, 0)) for c in chunks],
            out_specs=pl.BlockSpec((2, step, n_out, own_k, own_m), lambda i, w: (0, i, 0, 0, 0)),
            scratch_shapes=[pltpu.VMEM((n_out, own_k, own_m), f32)] * 2,
        ),
        out_shape=out,
        compiler_params=params(),
        cost_estimate=cost(6 * n_in * n_out * own_k * own_m, out, out),
        name="weight_grad",
    )(where, spec_all, *chunks)


def slabs_of(value, shape):
    high = lax.reduce_precision(value, 8, 7)
    parts = jnp.stack([high, value - high]).astype(bf16).reshape(-1)
    size = math.prod(shape)
    count = -(-parts.shape[0] // size)
    return jnp.pad(parts, (0, count * size - parts.shape[0])).reshape((count,) + shape)


def sum_of_slabs(slabs, shape):
    total = slabs.astype(f32).sum(axis=0).reshape(-1)
    return total[: 2 * math.prod(shape)].reshape((2,) + shape).sum(axis=0)


def on_device(n_gx, n_gy, state_in, tile_class, class_bias, w_point, spec_weight, grad_out):
    sizes = (n_gx, n_gy)
    n_grid = n_gx * n_gy
    own_chan, n_rows, n_cols = state_in.shape
    own_k, own_m = spec_weight.shape[3:]
    m_y, m_x = own_k * n_gx, own_m * n_gy
    n_x, n_y = n_rows * n_gx, n_cols * n_gy
    gx_index = lax.axis_index("gx")
    gy_index = lax.axis_index("gy")
    col_index = lax.axis_index("col")
    scale_fwd = 1.0 / math.sqrt(n_x * n_y)
    scale_inv = 1.0 / math.sqrt(2.0 * m_x * m_y)
    other = [(0, 1), (1, 0)]
    where = jnp.stack([col_index, gx_index]).astype(jnp.int32)

    state_other = lax.ppermute(state_in, "col", other)
    y_tab = y_table(n_y, m_y, gy_index * n_cols, n_cols)
    x_tab = x_table(n_x, m_x, own_m, gx_index * n_rows, n_rows)
    tables = (y_tab, x_tab)

    tile_rows, tile_cols = tile_class.shape
    one_hot = (tile_class[:, None, :] == jnp.arange(NCLASS, dtype=jnp.int32)[None, :, None]).astype(f32)
    widen = jnp.asarray(np.repeat(np.eye(tile_cols), TILE, axis=1).astype(np.float32))
    bias_own = lax.dynamic_slice_in_dim(class_bias, col_index * own_chan, own_chan, 1)
    tile_bias = jnp.sum(one_hot[:, :, None, :] * bias_own[None, :, :, None], axis=1)
    bias = jnp.dot(
        tile_bias.reshape(tile_rows * own_chan, tile_cols), widen, precision=lax.Precision.HIGHEST
    ).reshape(tile_rows, own_chan, n_cols)
    classes = jnp.dot(
        one_hot.astype(bf16).reshape(tile_rows * NCLASS, tile_cols), widen.astype(bf16), preferred_element_type=f32
    )
    classes = classes.astype(bf16).reshape(tile_rows, NCLASS, n_cols)
    mix, _ = point_mixing(where, [state_in, state_other], w_point, False, [bias])

    terms = exchange(forward_modes(where, state_in, tables, sizes, own_k))
    terms, mix = lax.optimization_barrier((terms, mix))
    spectrum = (terms.astype(f32).sum(axis=0) * scale_fwd).astype(bf16)
    spectrum_other = lax.ppermute(spectrum, "col", other)
    halves = SPLITS if own_chan % SPLITS == 0 else 1
    count = own_chan // halves
    mixed = [
        exchange(
            mix_modes(where, spec_weight, spectrum, spectrum_other, n_grid, scale_inv, n * count, count)
        )
        for n in range(halves)
    ]

    done = ()
    for n in range(halves):
        done = middle(where, mix, grad_out, tables, mixed[n], sizes, n * count, done)
    act_out, grad_pre, back_terms = done
    back_terms = [exchange(back_terms)]
    pre_other = lax.ppermute(grad_pre, "col", other)

    sums = cell_sums(where, grad_pre, state_in, state_other, classes, scale_fwd)
    first = col_index == 0
    spec_all = jnp.concatenate(
        [jnp.where(first, spectrum, spectrum_other), jnp.where(first, spectrum_other, spectrum)], axis=0
    )
    sums, spec_all, *back_terms = lax.optimization_barrier((sums, spec_all, *back_terms))

    input_terms = back_mix(where, spec_weight, back_terms, scale_inv, scale_fwd)
    input_modes = input_terms[own_chan:] + lax.ppermute(input_terms[:own_chan], "col", other)
    sent = jnp.concatenate([input_modes.astype(bf16), slabs_of(sums, input_modes.shape[1:])], axis=0)
    arrived = exchange(jnp.broadcast_to(sent[None], (n_grid,) + sent.shape))

    grad_spec = weight_grad(where, back_terms, spec_all, own_chan, scale_inv)
    point_back, mark = point_mixing(where, [grad_pre, pre_other], w_point, True)
    arrived, grad_spec, mark = lax.optimization_barrier((arrived, grad_spec, mark))

    grad_in = last(where, point_back, tables, arrived, sizes, mark)
    sums = sum_of_slabs(arrived[:, own_chan:], sums.shape)
    grad_point = sums[:, : 2 * own_chan]
    grad_bias = sums[:, 2 * own_chan : 2 * own_chan + NCLASS].T
    return (act_out, grad_in, grad_spec, grad_point, grad_bias)


def solution(mesh):
    return jax.shard_map(
        functools.partial(on_device, mesh.shape["gx"], mesh.shape["gy"]),
        mesh=mesh,
        in_specs=(
            P(("groups", "col"), "gx", "gy"),
            P(("groups", "gx"), "gy"),
            P(),
            P(),
            P(None, None, "col", "gx", "gy"),
            P(("groups", "col"), "gx", "gy"),
        ),
        out_specs=(
            P(("groups", "col"), "gx", "gy"),
            P(("groups", "col"), "gx", "gy"),
            P("groups", None, "col", "gx", "gy"),
            P(("groups", "col"), None),
            P("groups", "col"),
        ),
        check_vma=False,
    )
```
